256 devices in a mesh: va: 8 (over x, y_lo), vb: 8 (over z), aux: 4 (over y_hi, core).
Axes of the slice: x: 4, y: 4 (y_hi: 2, y_lo: 2; y = y_hi * 2 + y_lo), z: 8, core: 2. Of those that a mesh axis runs over, the one named last changes fastest.
Arguments:
- factors: float32 [1024, 8, 2048], P(None, None, 'va'), may hold values from -0.046875 to 0.046875
- domains: int32 [8, 16, 8], replicated, may hold values from 0 to 1, as said below
- occ_energy: float32 [8], replicated, may hold values from -3 to -0.5
- vir_energy: float32 [2048], replicated, may hold values from 0.5 to 3
Outputs:
- amplitudes: float32 [8, 2048, 8, 2048], P(None, 'va', 'aux', 'vb')
The draws below stay inside these ranges and needn't reach their ends.
Inputs may be any that keep to these rules, and one draw needn't show every extreme that they name: `domains`: for every occupied orbital and every block of 128 virtuals, exactly 6 of the 8 fitting blocks are 1.
All inputs are finite; a program needn't handle non-finite values.
Results may differ from the reference program's by a relative error of at most 0.000096.
Values sent between devices are 32-bit elements; how exact they have to be, the bound alone decides.
No kernel may reach another device: no remote copies, remote signals or barrier semaphores. Data moves between devices by JAX's collectives and lax.ppermute only.
A program may use at most 128 MiB of HBM per device.

```python
import math
import jax
import jax.numpy as jnp
from jax import lax

O = 8
V = 2048
NAUX = 1024
BLK = 128
PRESENT = 6
NVB = 16
NPB = 8


def draw_domains(key, part):
    scores = jax.random.randint(key, (O, NVB, NPB), 0, 1 << 20) * NPB + jnp.arange(NPB, dtype=jnp.int32)
    picks = lax.top_k(scores, PRESENT)[1]
    hits = (picks[..., None] == jnp.arange(NPB, dtype=jnp.int32)).astype(jnp.int32)
    return jnp.sum(hits, axis=-2).astype(jnp.int32)


def levels(key, extent, split, smallest, top_value):
    gain, own = 1.0, jax.random.fold_in(key, 6)
    for position, blocks in split:
        draws = jnp.exp(jax.random.uniform(jax.random.fold_in(own, position), (blocks,), jnp.float32, smallest / len(split), top_value / len(split)))
        gain = gain * jnp.repeat(draws, extent[position] // blocks).reshape([-1 if axis == position else 1 for axis in range(len(extent))])
    return gain


def scatter_about(own_key, extent, deviation, bound, shards=(), kind=jnp.bfloat16):
    entries = jax.random.normal(own_key, extent, jnp.float32) * deviation
    if len(shards) > 0:
        entries = levels(own_key, extent, shards, -0.22, 0.18) * entries
    return jnp.clip(entries, min=-bound, max=bound).astype(kind)


def setup_inputs(seed: int = 0) -> dict:
    key_of = jax.random.split(jax.random.key(seed), 5)
    return {
        "factors": scatter_about(key_of[0], (NAUX, O, V), (O * V) ** -0.5, 0.046875, ((2, 8),), jnp.float32),
        "domains": draw_domains(jax.random.fold_in(key_of[4], 71), 0),
        "occ_energy": jnp.clip(jax.random.uniform(key_of[2], (O,), jnp.float32, -3.0, -0.5), -3.0, -0.5),
        "vir_energy": jnp.clip(jax.random.uniform(key_of[3], (V,), jnp.float32, 0.5, 3.0), 0.5, 3.0),
    }


highest = lax.Precision.HIGHEST

def spread_mask(domains):
    expanded = jnp.transpose(domains, (2, 0, 1)).astype(jnp.float32)
    fit_blocks, orbitals, vir_blocks = expanded.shape
    expanded = jnp.broadcast_to(expanded[:, None, :, :, None], (fit_blocks, BLK, orbitals, vir_blocks, BLK))
    return expanded.reshape(fit_blocks * BLK, orbitals, vir_blocks * BLK)

def contract_first(left, right):
    return lax.dot_general(left, right, (((0,), (0,)), ((), ())), precision=highest, preferred_element_type=jnp.float32)

def reference(factors, domains, occ_energy, vir_energy):
    weights = spread_mask(domains)
    masked = factors * weights
    flattened = masked.reshape(NAUX, O * V)
    weight_flat = weights.reshape(NAUX, O * V)
    vir_pair = vir_energy[:, None, None] + vir_energy[None, None, :] - occ_energy[None, :, None]

    def block_denominator(index):
        return (vir_pair - occ_energy[index]).reshape(V, O * V)

    def first_block(index):
        rows = lax.dynamic_slice_in_dim(flattened, index * V, V, 1)
        direct_rows = contract_first(rows, flattened)
        first_rows = -direct_rows / block_denominator(index)
        dressed_rows = lax.dot_general(flattened, first_rows, (((1,), (1,)), ((), ())), precision=highest, preferred_element_type=jnp.float32)
        return (dressed_rows, direct_rows)
    indices = jnp.arange(O, dtype=jnp.int32)
    dressed_blocks, direct_blocks = lax.map(first_block, indices)
    dressed = jnp.transpose(dressed_blocks, (1, 0, 2)).reshape(NAUX, O * V) * weight_flat
    summed_factors = flattened + dressed

    def second_block(carried):
        index, direct_rows = carried
        rows_sum = lax.dynamic_slice_in_dim(summed_factors, index * V, V, 1)
        rows_dressed = lax.dynamic_slice_in_dim(dressed, index * V, V, 1)
        cross_rows = 2.0 * contract_first(rows_dressed, summed_factors)
        mirror_rows = 2.0 * contract_first(rows_sum, dressed)
        second_rows = -(direct_rows + cross_rows + mirror_rows) / block_denominator(index)
        return (second_rows * (8.0 * O * V / math.sqrt(NAUX))).reshape(V, O, V)
    return lax.map(second_block, (indices, direct_blocks))
```

```python
import math

import jax
import jax.numpy as jnp
from jax import lax
from jax.experimental import pallas as pl
from jax.experimental.pallas import tpu as pltpu
from jax.sharding import PartitionSpec as P

O = 8
V = 2048
NAUX = 1024
BLK = 128
NPB = 8
NVB = 16
SLOTS = 6
PRES = SLOTS * BLK
PIECE = PRES // 8
TILE = 256
SCALE = 8.0 * O * V / math.sqrt(NAUX)
AXES = ("va", "vb", "aux")
f32 = jnp.float32
bf16 = jnp.bfloat16


def route(move):
    pairs = []
    for a in range(8):
        for b in range(8):
            for c in range(4):
                A, B, C = move(a, b, c)
                pairs.append(((a * 8 + b) * 4 + c, (A * 8 + B) * 4 + C))
    return pairs


def shift_x(a, d):
    return ((a // 2 + d) % 4) * 2 + a % 2


def y_by_core(a, b, c):
    y = (c // 2) * 2 + a % 2
    y = (y + (1 if c % 2 == 0 else -1)) % 4
    return (a // 2) * 2 + y % 2, b, (y // 2) * 2 + c % 2


ROUTES = {
    "x+": route(lambda a, b, c: (shift_x(a, 1), b, c)),
    "x-": route(lambda a, b, c: (shift_x(a, -1), b, c)),
    "x2": route(lambda a, b, c: (shift_x(a, 2), b, c)),
    "y": route(y_by_core),
    "y_lo": route(lambda a, b, c: (a ^ 1, b, c)),
    "y_hi": route(lambda a, b, c: (a, b, c ^ 2)),
    "z+": route(lambda a, b, c: (a, (b + 1) % 8, c)),
    "z-": route(lambda a, b, c: (a, (b - 1) % 8, c)),
    "core": route(lambda a, b, c: (a, b, c ^ 1)),
    "turn": route(lambda a, b, c: (b, a, c)),
}


def send(value, way):
    return lax.ppermute(value, AXES, ROUTES[way])


def split(value):
    high = value.astype(bf16)
    low = (value - high.astype(f32)).astype(bf16)
    return high, low


def dot3(left, right, dims):
    def one(l, r):
        return lax.dot_general(l, r, (dims, ((), ())), preferred_element_type=f32)

    return one(left[0], right[0]) + (one(left[0], right[1]) + one(left[1], right[0]))


def present(domains, orbital, block, fit):
    return domains[(orbital * NVB + block) * NPB + fit]


def prepare_kernel(meta, domains, x, column, rows_high, rows_low, piece, packed):
    a, z, c = meta[0], meta[1], meta[2]
    core = lax.rem(c, 2)

    def load(fit, orbital, half):
        return x[half, pl.ds(fit * BLK * O + orbital, BLK, stride=O), :]

    def pack(target, orbital, half):
        slot = jnp.int32(0)
        for fit in range(NPB):
            here = present(domains, orbital, 2 * a + half, fit)

            @pl.when(here == 1)
            def _(slot=slot, fit=fit):
                target[pl.ds(pl.multiple_of(slot * BLK, BLK), BLK), :] = load(fit, orbital, half)

            slot = slot + here

    pack(column, z, core)
    for e in range(2):
        for half in range(2):
            store = packed.at[2 * e + half]
            pack(store, 2 * c + e, half)
            window = pl.ds(pl.multiple_of(z * PIECE, 8), PIECE)
            piece[e, :, half * BLK : (half + 1) * BLK] = store[window, :]
    for r in range(4):
        orbital = 2 * c + r if r < 2 else 2 * (c + 1 - 2 * core) + r - 2
        for half in range(2):
            for fit in range(NPB):
                here = present(domains, orbital, 2 * a + half, fit).astype(f32)
                high, low = split(load(fit, orbital, half) * here)
                place = (pl.ds(fit * BLK, BLK), pl.ds(r * TILE + half * BLK, BLK))
                rows_high[place] = high
                rows_low[place] = low


def half_spec():
    return pl.BlockSpec(memory_space=pltpu.VMEM)


def prepare(meta, domains, factors):
    smem = pl.BlockSpec(memory_space=pltpu.SMEM)
    vmem = pl.BlockSpec(memory_space=pltpu.VMEM)

    def kernel(meta, domains, factors, column, rows_high, rows_low, piece, packed, halves, sems):
        copies = []
        for half in range(2):
            copies.append(
                pltpu.make_async_copy(
                    factors.at[:, pl.ds(half * BLK, BLK)], halves.at[half], sems.at[half]
                )
            )
            copies[-1].start()
        for copy in copies:
            copy.wait()
        prepare_kernel(meta, domains, halves, column, rows_high, rows_low, piece, packed)

    return pl.pallas_call(
        kernel,
        out_shape=(
            jax.ShapeDtypeStruct((PRES, BLK), f32),
            jax.ShapeDtypeStruct((NAUX, 4 * TILE), bf16),
            jax.ShapeDtypeStruct((NAUX, 4 * TILE), bf16),
            jax.ShapeDtypeStruct((2, PIECE, TILE), f32),
        ),
        in_specs=[smem, smem, pl.BlockSpec(memory_space=pl.ANY)],
        out_specs=(vmem, vmem, vmem, vmem),
        scratch_shapes=[
            pltpu.VMEM((4, PRES, BLK), f32),
            pltpu.VMEM((2, NAUX * O, BLK), f32),
            pltpu.SemaphoreType.DMA((2,)),
        ],
        compiler_params=pltpu.CompilerParams(vmem_limit_bytes=40 * 1024 * 1024),
        cost_estimate=pl.CostEstimate(flops=0, bytes_accessed=24 * 1024 * 1024, transcendentals=0),
        name="prepare",
    )(meta, domains, factors.reshape(NAUX * O, TILE))


def dress(meta, domains, rows, row_energy, column_energy, blocks, tiles, total, last):
    count = len(blocks)
    width = count * BLK
    has_total = total is not None
    smem = pl.BlockSpec(memory_space=pltpu.SMEM)
    vmem = pl.BlockSpec(memory_space=pltpu.VMEM)

    def kernel(*refs):
        meta, tile_of, domains, rows_high, rows_low, row_energy, column_energy = refs[:7]
        columns = refs[7 : 7 + count]
        refs = refs[7 + count :]
        if has_total:
            total, refs = refs[0], refs[1:]
        if last:
            keep, give, high, low, packed = refs
        else:
            out, high, low = refs
        a, z, c = meta[0], meta[1], meta[2]
        core = lax.rem(c, 2)
        for q in range(count):
            slot = jnp.int32(0)
            lanes = slice(q * BLK, (q + 1) * BLK)
            for fit in range(NPB):
                here = present(domains, z, 2 * tile_of[q] + core, fit)
                block = columns[q][pl.ds(pl.multiple_of(jnp.minimum(slot, SLOTS - 1) * BLK, BLK), BLK), :]
                block = jnp.where(here == 1, block, 0.0)
                one, two = split(block)
                high[fit * BLK : (fit + 1) * BLK, lanes] = one
                low[fit * BLK : (fit + 1) * BLK, lanes] = two
                slot = slot + here
        for r in range(4):
            span = slice(r * TILE, (r + 1) * TILE)
            direct = dot3(
                (high[...], low[...]), (rows_high[:, span], rows_low[:, span]), ((0,), (0,))
            )
            amps = -direct / (column_energy[...] + row_energy[:, span])
            found = dot3((high[...], low[...]), split(amps), ((1,), (0,)))
            if has_total:
                found = found + total[:, span]
            if not last:
                out[:, span] = found
                continue
            target, e = (keep, r) if r < 2 else (give, r - 2)
            orbital = 2 * c + r if r < 2 else 2 * (c + 1 - 2 * core) + r - 2
            for half in range(2):
                lanes = slice(half * BLK, (half + 1) * BLK)
                slot = jnp.int32(0)
                for fit in range(NPB):
                    here = present(domains, orbital, 2 * a + half, fit)

                    @pl.when(here == 1)
                    def _(slot=slot, fit=fit, lanes=lanes):
                        packed[r, pl.ds(pl.multiple_of(slot * BLK, BLK), BLK), lanes] = found[
                            fit * BLK : (fit + 1) * BLK, lanes
                        ]

                    slot = slot + here
            for o in range(8):
                place = lax.rem(z + o, 8)
                target[o, e] = packed[r, pl.ds(pl.multiple_of(place * PIECE, 8), PIECE), :]

    if last:
        shape = jax.ShapeDtypeStruct((8, 2, PIECE, TILE), f32)
        out_shape, out_specs = (shape, shape), (vmem, vmem)
    else:
        out_shape, out_specs = jax.ShapeDtypeStruct((NAUX, 4 * TILE), f32), vmem
    scratch = [pltpu.VMEM((NAUX, width), bf16), pltpu.VMEM((NAUX, width), bf16)]
    if last:
        scratch.append(pltpu.VMEM((4, PRES, TILE), f32))
    operands = [meta, tiles, domains, *rows, row_energy, column_energy, *blocks]
    in_specs = [smem] * 3 + [vmem] * (4 + count)
    if has_total:
        operands.append(total)
        in_specs.append(vmem)
    work = 12 * NAUX * width * 4 * TILE
    return pl.pallas_call(
        kernel,
        out_shape=out_shape,
        in_specs=in_specs,
        out_specs=out_specs,
        scratch_shapes=scratch,
        compiler_params=pltpu.CompilerParams(vmem_limit_bytes=48 * 1024 * 1024),
        cost_estimate=pl.CostEstimate(flops=work, bytes_accessed=16 * 1024 * 1024, transcendentals=0),
        name="dress_last" if last else "dress",
    )(*operands)


def finish(meta, domains, occ_energy, vir_near, col_energy, far, near):
    smem = pl.BlockSpec(memory_space=pltpu.SMEM)
    vmem = pl.BlockSpec(memory_space=pltpu.VMEM)
    far_parts, far_arrays = far
    near_parts, near_arrays = near
    n_far, n_near = len(far_arrays), len(near_arrays)

    def kernel(*refs):
        meta, domains, occ, vir_near, col_energy = refs[:5]
        far_refs = refs[5 : 5 + n_far]
        near_refs = refs[5 + n_far : 5 + n_far + n_near]
        out, packed, far_high, far_low, high, low = refs[5 + n_far + n_near :]
        a, z, c = meta[0], meta[1], meta[2]

        def spread(store, orbital, first_block, into_high, into_low, start):
            for half in range(2):
                slot = jnp.int32(0)
                lanes = slice(half * BLK, (half + 1) * BLK)
                wide = slice(start + half * BLK, start + (half + 1) * BLK)
                for fit in range(NPB):
                    here = present(domains, orbital, first_block + half, fit)
                    block = store[pl.ds(pl.multiple_of(jnp.minimum(slot, SLOTS - 1) * BLK, BLK), BLK), lanes]
                    block = jnp.where(here == 1, block, 0.0)
                    one, two = split(block)
                    into_high[fit * BLK : (fit + 1) * BLK, wide] = one
                    into_low[fit * BLK : (fit + 1) * BLK, wide] = two
                    slot = slot + here

        def rows_of(place):
            return pl.ds(pl.multiple_of(place * PIECE, 8), PIECE)

        for e in range(2):
            for offset, flip, which, part in far_parts:
                place = jnp.bitwise_xor(lax.rem(a + offset, 8), flip)
                packed.at[e][rows_of(place), :] = far_refs[which][part + (e,)]
            spread(packed.at[e], 2 * c + e, 2 * z, far_high, far_low, e * TILE)
        for g in range(4):
            pair = jnp.bitwise_xor(c, g)
            for e in range(2):
                orbital = 2 * pair + e
                store = packed.at[2 + 2 * g + e]
                for offset, which, part in near_parts[g]:
                    store[rows_of(lax.rem(z + offset, 8)), :] = near_refs[which][part + (e,)]
                spread(store, orbital, 2 * a, high, low, 0)
                residual = dot3(
                    (high[...], low[...]), (far_high[...], far_low[...]), ((0,), (0,))
                )
                energy = (vir_near[...] - occ[orbital]) + col_energy[...]
                result = (residual * (-SCALE)) / energy
                out[orbital, :, 0, :] = result[:, :TILE]
                out[orbital, :, 1, :] = result[:, TILE:]

    return pl.pallas_call(
        kernel,
        out_shape=jax.ShapeDtypeStruct((O, TILE, 2, TILE), f32),
        in_specs=[smem] * 3 + [vmem] * (2 + n_far + n_near),
        out_specs=vmem,
        scratch_shapes=[
            pltpu.VMEM((10, PRES, TILE), f32),
            pltpu.VMEM((NAUX, 2 * TILE), bf16),
            pltpu.VMEM((NAUX, 2 * TILE), bf16),
            pltpu.VMEM((NAUX, TILE), bf16),
            pltpu.VMEM((NAUX, TILE), bf16),
        ],
        compiler_params=pltpu.CompilerParams(vmem_limit_bytes=48 * 1024 * 1024),
        cost_estimate=pl.CostEstimate(
            flops=6 * NAUX * 2048 * 512, bytes_accessed=16 * 1024 * 1024, transcendentals=0
        ),
        name="finish",
    )(meta, domains, occ_energy, vir_near, col_energy, *far_arrays, *near_arrays)


def body(factors, domains, occ_energy, vir_energy):
    a = lax.axis_index("va")
    z = lax.axis_index("vb")
    c = lax.axis_index("aux")
    core = c % 2
    meta = jnp.stack([a, z, c]).astype(jnp.int32)
    flags = domains.reshape(-1)
    column, rows_high, rows_low, piece = prepare(meta, flags, factors)
    rows = (rows_high, rows_low)

    vir_near = lax.dynamic_slice_in_dim(vir_energy, a * TILE, TILE)
    occ_pairs = occ_energy.reshape(4, 2)
    occ_rows = jnp.concatenate([occ_pairs[c], occ_pairs[c ^ 1]])
    row_energy = (vir_near[None, :] - occ_rows[:, None]).reshape(1, 4 * TILE)
    vir_blocks = vir_energy.reshape(8, 2, BLK)[:, core] - occ_energy[z]
    own = jnp.stack([a, (a + 6) % 8, (a + 2) % 8, (a + 4) % 8]).astype(jnp.int32)
    other = own ^ 1

    def energies(tiles):
        return vir_blocks[tiles].reshape(-1, 1)

    here = [column, send(column, "x+"), send(column, "x-"), send(column, "x2")]
    there = [send(block, "y") for block in here]
    total = dress(meta, flags, rows, row_energy, energies(own), here, own, None, False)
    keep, give = dress(meta, flags, rows, row_energy, energies(other), there, other, total, True)

    first = send(give[3:5], "core")
    rest = send(jnp.concatenate([give[:3], give[5:]]), "core")
    got = [rest[0], rest[1], rest[2], first[0], first[1], rest[3], rest[4], rest[5]]
    plus = send(keep[3] + got[3], "z+")
    minus = send(keep[4] + got[4], "z-")
    minus = send(keep[5] + got[5] + minus, "z-")
    plus = send(keep[2] + got[2] + plus, "z+")
    minus = send(keep[6] + got[6] + minus, "z-")
    plus = send(keep[1] + got[1] + plus, "z+")
    minus = send(keep[7] + got[7] + minus, "z-")
    summed = (keep[0] + got[0]) + (plus + minus)
    combined = piece + 2.0 * summed

    turned = send(combined, "turn")
    far_pair = jnp.stack([turned, send(turned, "y_lo")])
    far_arrays = [far_pair, send(far_pair, "x+"), send(far_pair, "x-"), send(far_pair, "x2")]
    far_parts = []
    for which, offset in enumerate([0, 6, 2, 4]):
        far_parts += [(offset, 0, which, (0,)), (offset, 1, which, (1,))]

    both = jnp.stack([combined, send(combined, "y_hi")])
    plus1, minus1 = send(both, "z+"), send(both, "z-")
    plus2, minus2 = send(plus1, "z+"), send(minus1, "z-")
    plus3, minus3 = send(plus2, "z+"), send(minus2, "z-")
    plus4, minus4 = send(plus3[0], "z+"), send(minus3[1], "z-")
    ring = [both, plus1, minus1, plus2, minus2, plus3, minus3, plus4, minus4]
    swapped = [send(part, "core") for part in ring]
    near_arrays = ring + swapped
    near_parts = []
    for g in range(4):
        base = 0 if g % 2 == 0 else len(ring)
        upper = g // 2
        parts = [(o, base + n, (upper,)) for n, o in enumerate([0, 7, 1, 6, 2, 5, 3])]
        parts.append((4, base + 7 + upper, ()))
        near_parts.append(parts)
    pair_energy = lax.dynamic_slice_in_dim(vir_energy, z * TILE, TILE)[None, :] - occ_pairs[c][:, None]
    return finish(
        meta,
        flags,
        occ_energy,
        vir_near.reshape(TILE, 1),
        pair_energy.reshape(1, 2 * TILE),
        (far_parts, far_arrays),
        (near_parts, near_arrays),
    )


def solution(mesh):
    placed = (P(None, None, "va"), P(), P(), P())
    return jax.shard_map(
        body, mesh=mesh, in_specs=placed, out_specs=P(None, "va", "aux", "vb"), check_vma=False
    )
```

```python
import math

import jax
import jax.numpy as jnp
from jax import lax
from jax.experimental import pallas as pl
from jax.experimental.pallas import tpu as pltpu
from jax.sharding import PartitionSpec as P

O = 8
V = 2048
NAUX = 1024
BLK = 128
NPB = 8
NVB = 16
SLOTS = 6
PRES = SLOTS * BLK
PIECE = PRES // 8
TILE = 256
SCALE = 8.0 * O * V / math.sqrt(NAUX)
AXES = ("va", "vb", "aux")
f32 = jnp.float32
bf16 = jnp.bfloat16


def route(move):
    pairs = []
    for a in range(8):
        for b in range(8):
            for c in range(4):
                A, B, C = move(a, b, c)
                pairs.append(((a * 8 + b) * 4 + c, (A * 8 + B) * 4 + C))
    return pairs


def shift_x(a, d):
    return ((a // 2 + d) % 4) * 2 + a % 2


def y_by_core(a, b, c):
    y = (c // 2) * 2 + a % 2
    y = (y + (1 if c % 2 == 0 else -1)) % 4
    return (a // 2) * 2 + y % 2, b, (y // 2) * 2 + c % 2


ROUTES = {
    "x+": route(lambda a, b, c: (shift_x(a, 1), b, c)),
    "x-": route(lambda a, b, c: (shift_x(a, -1), b, c)),
    "x2": route(lambda a, b, c: (shift_x(a, 2), b, c)),
    "y": route(y_by_core),
    "y_lo": route(lambda a, b, c: (a ^ 1, b, c)),
    "y_hi": route(lambda a, b, c: (a, b, c ^ 2)),
    "z+": route(lambda a, b, c: (a, (b + 1) % 8, c)),
    "z-": route(lambda a, b, c: (a, (b - 1) % 8, c)),
    "core": route(lambda a, b, c: (a, b, c ^ 1)),
    "turn": route(lambda a, b, c: (b, a, c)),
}


def send(value, way):
    return lax.ppermute(value, AXES, ROUTES[way])


def split(value):
    high = value.astype(bf16)
    low = (value - high.astype(f32)).astype(bf16)
    return high, low


def dot3(left, right, dims):
    def one(l, r):
        return lax.dot_general(l, r, (dims, ((), ())), preferred_element_type=f32)

    return one(left[0], right[0]) + (one(left[0], right[1]) + one(left[1], right[0]))


def present(domains, orbital, block, fit):
    return domains[(orbital * NVB + block) * NPB + fit]


SMEM = pl.BlockSpec(memory_space=pltpu.SMEM)
VMEM = pl.BlockSpec(memory_space=pltpu.VMEM)


def params(mib, grid=0):
    order = {"dimension_semantics": ("arbitrary",) * grid} if grid else {}
    return pltpu.CompilerParams(vmem_limit_bytes=mib * 1024 * 1024, **order)


def cost(flops, mib):
    return pl.CostEstimate(flops=flops, bytes_accessed=mib * 1024 * 1024, transcendentals=0)


def block_rows(slot):
    return pl.ds(pl.multiple_of(slot * BLK, BLK), BLK)


def load(x, fit, orbital):
    return x[pl.ds(fit * BLK * O + orbital, BLK, stride=O), :]


def pack(target, x, domains, orbital, block):
    slot = jnp.int32(0)
    for fit in range(NPB):
        here = present(domains, orbital, block, fit)

        @pl.when(here == 1)
        def _(slot=slot, fit=fit):
            target[block_rows(slot), :] = load(x, fit, orbital)

        slot = slot + here


def pick_column(meta, domains, factors):
    def kernel(meta, domains, x, column):
        pack(column, x, domains, meta[1], 2 * meta[0] + lax.rem(meta[2], 2))

    return pl.pallas_call(
        kernel,
        out_shape=jax.ShapeDtypeStruct((PRES, BLK), f32),
        grid_spec=pltpu.PrefetchScalarGridSpec(
            num_scalar_prefetch=2,
            grid=(1,),
            in_specs=[pl.BlockSpec((NAUX * O, BLK), lambda n, meta, domains: (0, lax.rem(meta[2], 2)))],
            out_specs=pl.BlockSpec((PRES, BLK), lambda n, meta, domains: (0, 0)),
        ),
        compiler_params=params(56, 1),
        cost_estimate=cost(0, 5),
        name="pick_column",
    )(meta, domains, factors)


def prepare(meta, domains, factors):
    def kernel(meta, domains, x, rows_high, rows_low, piece, packed):
        a, z, c = meta[0], meta[1], meta[2]
        core = lax.rem(c, 2)
        for h in range(2):

            @pl.when(pl.program_id(0) == h)
            def _(h=h):
                lanes = slice(h * BLK, (h + 1) * BLK)
                for e in range(2):
                    store = packed.at[2 * e + h]
                    pack(store, x, domains, 2 * c + e, 2 * a + h)
                for r in range(4):
                    orbital = 2 * c + r if r < 2 else 2 * (c + 1 - 2 * core) + r - 2
                    for fit in range(NPB):
                        here = present(domains, orbital, 2 * a + h, fit).astype(f32)
                        high, low = split(load(x, fit, orbital) * here)
                        place = (slice(fit * BLK, (fit + 1) * BLK), slice(r * TILE + h * BLK, r * TILE + (h + 1) * BLK))
                        rows_high[place] = high
                        rows_low[place] = low
                window = pl.ds(pl.multiple_of(z * PIECE, 8), PIECE)
                for e in range(2):
                    piece[e, :, lanes] = packed[2 * e + h, window, :]

    return pl.pallas_call(
        kernel,
        out_shape=(
            jax.ShapeDtypeStruct((NAUX, 4 * TILE), bf16),
            jax.ShapeDtypeStruct((NAUX, 4 * TILE), bf16),
            jax.ShapeDtypeStruct((2, PIECE, TILE), f32),
        ),
        grid_spec=pltpu.PrefetchScalarGridSpec(
            num_scalar_prefetch=2,
            grid=(2,),
            in_specs=[pl.BlockSpec((NAUX * O, BLK), lambda n, meta, domains: (0, n))],
            out_specs=(
                pl.BlockSpec((NAUX, 4 * TILE), lambda n, meta, domains: (0, 0)),
                pl.BlockSpec((NAUX, 4 * TILE), lambda n, meta, domains: (0, 0)),
                pl.BlockSpec((2, PIECE, TILE), lambda n, meta, domains: (0, 0, 0)),
            ),
            scratch_shapes=[pltpu.VMEM((4, PRES, BLK), f32)],
        ),
        compiler_params=params(56, 1),
        cost_estimate=cost(0, 14),
        name="prepare",
    )(meta, domains, factors)


def tile_at(a, step):
    offset, flip = step
    return jnp.bitwise_xor(lax.rem(a + offset, 8), flip)


def dress(meta, domains, rows, row_energy, column_energy, blocks, steps, total, chunks, last):
    count = len(blocks)
    width = count * BLK
    has_total = total is not None

    def kernel(*refs):
        meta, domains, rows_high, rows_low, row_energy, column_energy = refs[:6]
        columns = refs[6 : 6 + count]
        refs = refs[6 + count :]
        before = None
        if has_total:
            before, refs = refs[0], refs[1:]
        out, wide, turned_high, turned_low = refs[:4]
        a, z, c = meta[0], meta[1], meta[2]
        core = lax.rem(c, 2)
        for q in range(count):
            slot = jnp.int32(0)
            span = slice(q * BLK, (q + 1) * BLK)
            for fit in range(NPB):
                here = present(domains, z, 2 * tile_at(a, steps[q]) + core, fit)
                block = columns[q][block_rows(jnp.minimum(slot, SLOTS - 1)), :]
                block = jnp.where(here == 1, block, 0.0)
                one, two = split(block)
                own = slice(fit * BLK, (fit + 1) * BLK)
                wide[own, q * BLK : (q + 1) * BLK] = one
                wide[own, width + q * BLK : width + (q + 1) * BLK] = one
                wide[own, 2 * width + q * BLK : 2 * width + (q + 1) * BLK] = two
                one, two = split(block.T)
                turned_high[span, own] = one
                turned_low[span, own] = two
                slot = slot + here
        for n, r in enumerate(chunks):
            span = slice(r * TILE, (r + 1) * TILE)
            direct = dot3(
                (turned_high[...], turned_low[...]), (rows_high[:, span], rows_low[:, span]), ((1,), (0,))
            )
            amps = -direct / (column_energy[...] + row_energy[:, span])
            high, low = split(amps)
            found = lax.dot_general(
                wide[...],
                jnp.concatenate([high, low, high], axis=0),
                (((1,), (0,)), ((), ())),
                preferred_element_type=f32,
            )
            if has_total:
                found = found + before[:, span]
            if not last:
                out[:, span] = found
                continue
            dense = refs[4].at[n]
            dense[...] = found
            orbital = 2 * c + r if r < 2 else 2 * (c + 1 - 2 * core) + r - 2
            for half in range(2):
                lanes = slice(half * BLK, (half + 1) * BLK)
                fits = [jnp.int32(0)] * SLOTS
                slot = jnp.int32(0)
                for fit in range(NPB):
                    here = present(domains, orbital, 2 * a + half, fit)
                    for s in range(SLOTS):
                        fits[s] = jnp.where((here == 1) & (slot == s), fit, fits[s])
                    slot = slot + here
                for k in range(24):
                    o = lax.rem(k // 3 + 8 - z, 8)
                    source = pl.ds(pl.multiple_of(fits[k // 4] * BLK + (k % 4) * 32, 32), 32)
                    out[o, n, (k % 3) * 32 : (k % 3 + 1) * 32, lanes] = dense[source, lanes]

    scratch = [
        pltpu.VMEM((NAUX, 3 * width), bf16),
        pltpu.VMEM((width, NAUX), bf16),
        pltpu.VMEM((width, NAUX), bf16),
    ]
    if last:
        out_shape = jax.ShapeDtypeStruct((8, len(chunks), PIECE, TILE), f32)
        scratch.append(pltpu.VMEM((len(chunks), NAUX, TILE), f32))
    else:
        out_shape = jax.ShapeDtypeStruct((NAUX, 4 * TILE), f32)
    operands = [meta, domains, *rows, row_energy, column_energy, *blocks]
    in_specs = [SMEM] * 2 + [VMEM] * (4 + count)
    if has_total:
        operands.append(total)
        in_specs.append(VMEM)
    return pl.pallas_call(
        kernel,
        out_shape=out_shape,
        in_specs=in_specs,
        out_specs=VMEM,
        scratch_shapes=scratch,
        compiler_params=params(32),
        cost_estimate=cost(12 * NAUX * width * len(chunks) * TILE, 14),
        name="dress",
    )(*operands)


def finish(meta, domains, occ_energy, vir_near, col_energy, far, near, groups, filled):
    far_parts, far_arrays = far
    near_parts, near_arrays = near
    n_far, n_near = len(far_arrays), len(near_arrays)
    has_filled = filled is not None

    def kernel(*refs):
        meta, domains, occ, vir_near, col_energy = refs[:5]
        far_refs = refs[5 : 5 + n_far]
        near_refs = refs[5 + n_far : 5 + n_far + n_near]
        refs = refs[5 + n_far + n_near + (1 if has_filled else 0) :]
        out, packed, far_packed, far_high, far_low, high, low = refs
        a, z, c = meta[0], meta[1], meta[2]
        step = pl.program_id(0)
        upper, e = step // 2, lax.rem(step, 2)

        def rows_of(place):
            return pl.ds(pl.multiple_of(place * PIECE, 8), PIECE)

        def blocks_of(store, orbital, first_block, put):
            for half in range(2):
                slot = jnp.int32(0)
                lanes = slice(half * BLK, (half + 1) * BLK)
                for fit in range(NPB):
                    here = present(domains, orbital, first_block + half, fit)
                    block = store[block_rows(jnp.minimum(slot, SLOTS - 1)), lanes]
                    put(half, fit, jnp.where(here == 1, block, 0.0))
                    slot = slot + here

        @pl.when(step == 0)
        def _():
            for f in range(2):
                for where, which, part in far_parts:
                    far_packed.at[f][rows_of(tile_at(a, where)), :] = far_refs[which][part + (f,)]

                def put(half, fit, block, f=f):
                    own = slice(fit * BLK, (fit + 1) * BLK)
                    lanes = slice(f * TILE + half * BLK, f * TILE + (half + 1) * BLK)
                    far_high[own, lanes], far_low[own, lanes] = split(block)

                blocks_of(far_packed.at[f], 2 * c + f, 2 * z, put)

        orbital = 2 * jnp.bitwise_xor(c, groups[0] + upper * (groups[1] - groups[0])) + e
        for offset, which, part in near_parts:
            place = rows_of(lax.rem(z + offset, 8))
            if part is not None:
                packed[place, :] = near_refs[which][part + (upper, e)]
                continue
            for n, (w, p) in enumerate(which):

                @pl.when(upper == n)
                def _(w=w, p=p, place=place):
                    packed[place, :] = near_refs[w][p + (e,)]

        def put(half, fit, block):
            own = slice(fit * BLK, (fit + 1) * BLK)
            span = slice(half * BLK, (half + 1) * BLK)
            high[span, own], low[span, own] = split(block.T)

        blocks_of(packed, orbital, 2 * a, put)
        residual = dot3((high[...], low[...]), (far_high[...], far_low[...]), ((1,), (0,)))
        energy = (vir_near[...] - occ[orbital]) + col_energy[...]
        result = (residual * (-SCALE)) / energy
        out[0, :, 0, :] = result[:, :TILE]
        out[0, :, 1, :] = result[:, TILE:]

    def place(n, meta, domains, occ):
        pair = jnp.bitwise_xor(meta[2], groups[0] + (n // 2) * (groups[1] - groups[0]))
        return 2 * pair + lax.rem(n, 2), 0, 0, 0

    operands = [meta, domains, occ_energy, vir_near, col_energy, *far_arrays, *near_arrays]
    in_specs = [VMEM] * (2 + n_far + n_near)
    aliases = {}
    if has_filled:
        aliases = {len(operands): 0}
        operands.append(filled)
        in_specs.append(pl.BlockSpec(memory_space=pl.ANY))
    return pl.pallas_call(
        kernel,
        out_shape=jax.ShapeDtypeStruct((O, TILE, 2, TILE), f32),
        grid_spec=pltpu.PrefetchScalarGridSpec(
            num_scalar_prefetch=3,
            grid=(4,),
            in_specs=in_specs,
            out_specs=pl.BlockSpec((1, TILE, 2, TILE), place),
            scratch_shapes=[
                pltpu.VMEM((PRES, TILE), f32),
                pltpu.VMEM((2, PRES, TILE), f32),
                pltpu.VMEM((NAUX, 2 * TILE), bf16),
                pltpu.VMEM((NAUX, 2 * TILE), bf16),
                pltpu.VMEM((TILE, NAUX), bf16),
                pltpu.VMEM((TILE, NAUX), bf16),
            ],
        ),
        input_output_aliases=aliases,
        compiler_params=params(56, 1),
        cost_estimate=cost(6 * NAUX * 1024 * 512, 8),
        name="finish",
    )(*operands)


def body(factors, domains, occ_energy, vir_energy):
    a = lax.axis_index("va")
    z = lax.axis_index("vb")
    c = lax.axis_index("aux")
    core = c % 2
    meta = jnp.stack([a, z, c]).astype(jnp.int32)
    flags = domains.reshape(-1)
    flat = factors.reshape(NAUX * O, TILE)

    column = pick_column(meta, flags, flat)
    right, left, beyond = send(column, "x+"), send(column, "x-"), send(column, "x2")
    y_own, y_right, y_left = (send(block, "y") for block in (column, right, left))
    rows_high, rows_low, piece = prepare(meta, flags, flat)
    rows = (rows_high, rows_low)
    vir_near = lax.dynamic_slice_in_dim(vir_energy, a * TILE, TILE)
    occ_pairs = occ_energy.reshape(4, 2)
    occ_rows = jnp.concatenate([occ_pairs[c], occ_pairs[c ^ 1]])
    row_energy = (vir_near[None, :] - occ_rows[:, None]).reshape(1, 4 * TILE)
    tiles = jnp.stack([(a + d) % 8 ^ f for d, f in ((0, 0), (0, 1), (6, 0), (2, 0), (6, 1), (2, 1), (4, 0), (4, 1))])
    energies = (vir_energy.reshape(8, 2, BLK)[:, core][tiles] - occ_energy[z]).reshape(8 * BLK, 1)

    def add(n, blocks, steps, total, chunks=(0, 1, 2, 3), last=False):
        part = energies[2 * n * BLK : 2 * (n + 1) * BLK]
        return dress(meta, flags, rows, row_energy, part, blocks, steps, total, chunks, last)

    total = add(0, [column, y_own], [(0, 0), (0, 1)], None)
    ready, total = lax.optimization_barrier((beyond, total))
    y_beyond = send(ready, "y")
    total = add(1, [right, left], [(6, 0), (2, 0)], total)
    total = add(2, [y_right, y_left], [(6, 1), (2, 1)], total)
    final = ([beyond, y_beyond], [(4, 0), (4, 1)], total)
    give = add(3, *final, chunks=(2, 3), last=True)

    first = send(give[3:5], "core")
    rest = send(jnp.concatenate([give[:3], give[5:]]), "core")
    keep = add(3, *final, chunks=(0, 1), last=True)
    got = [rest[0], rest[1], rest[2], first[0], first[1], rest[3], rest[4], rest[5]]
    plus = send(keep[3] + got[3], "z+")
    minus = send(keep[4] + got[4], "z-")
    minus = send(keep[5] + got[5] + minus, "z-")
    plus = send(keep[2] + got[2] + plus, "z+")
    minus = send(keep[6] + got[6] + minus, "z-")
    plus = send(keep[1] + got[1] + plus, "z+")
    minus = send(keep[7] + got[7] + minus, "z-")
    summed = (keep[0] + got[0]) + (plus + minus)
    combined = piece + 2.0 * summed

    turned = send(combined, "turn")
    across = send(combined, "y_hi")
    combined, turned, across = lax.optimization_barrier((combined, turned, across))
    both = jnp.stack([combined, across])
    plus1, minus1 = send(both, "z+"), send(both, "z-")
    far_pair = jnp.stack([turned, send(turned, "y_lo")])

    plus1, minus1, far_pair = lax.optimization_barrier((plus1, minus1, far_pair))
    far_right, far_left = send(far_pair, "x+"), send(far_pair, "x-")
    plus2, minus2 = send(plus1, "z+"), send(minus1, "z-")
    plus2, minus2, far_right, far_left = lax.optimization_barrier((plus2, minus2, far_right, far_left))
    far_beyond = send(far_pair, "x2")
    plus3, minus3 = send(plus2, "z+"), send(minus2, "z-")
    plus3, minus3, far_beyond = lax.optimization_barrier((plus3, minus3, far_beyond))
    far_arrays = [far_pair, far_right, far_left, far_beyond]
    far_parts = []
    for which, offset in enumerate([0, 6, 2, 4]):
        far_parts += [((offset, 0), which, (0,)), ((offset, 1), which, (1,))]
    early = send(jnp.stack([both, plus1, minus1, plus2, minus2]), "core")
    plus4, minus4 = send(plus3[0], "z+"), send(minus3[1], "z-")
    late = send(jnp.stack([plus3, minus3, jnp.stack([plus4, minus4])]), "core")
    ring = [both, plus1, minus1, plus2, minus2, plus3, minus3, plus4, minus4]
    offsets = [0, 7, 1, 6, 2, 5, 3]
    ring_parts = [(o, n, ()) for n, o in enumerate(offsets)] + [(4, ((7, ()), (8, ())), None)]
    swap_parts = [(o, 0, (n,)) if n < 5 else (o, 1, (n - 5,)) for n, o in enumerate(offsets)] + [(4, 1, (2,))]
    pair_energy = lax.dynamic_slice_in_dim(vir_energy, z * TILE, TILE)[None, :] - occ_pairs[c][:, None]

    def rows_for(near, groups, filled):
        return finish(
            meta,
            flags,
            occ_energy,
            vir_near.reshape(TILE, 1),
            pair_energy.reshape(1, 2 * TILE),
            (far_parts, far_arrays),
            near,
            groups,
            filled,
        )

    filled = rows_for((ring_parts, ring), (0, 2), None)
    return rows_for((swap_parts, [early, late]), (1, 3), filled)


def solution(mesh):
    placed = (P(None, None, "va"), P(), P(), P())
    return jax.shard_map(
        body, mesh=mesh, in_specs=placed, out_specs=P(None, "va", "aux", "vb"), check_vma=False
    )
```

```python
import math

import jax
import jax.numpy as jnp
from jax import lax
from jax.experimental import pallas as pl
from jax.experimental.pallas import tpu as pltpu
from jax.sharding import PartitionSpec as P

O = 8
V = 2048
NAUX = 1024
BLK = 128
NPB = 8
NVB = 16
SLOTS = 6
PRES = SLOTS * BLK
PIECE = PRES // 8
TILE = 256
SCALE = 8.0 * O * V / math.sqrt(NAUX)
AXES = ("va", "vb", "aux")
f32 = jnp.float32
bf16 = jnp.bfloat16


def route(move):
    pairs = []
    for a in range(8):
        for b in range(8):
            for c in range(4):
                A, B, C = move(a, b, c)
                pairs.append(((a * 8 + b) * 4 + c, (A * 8 + B) * 4 + C))
    return pairs


def shift_x(a, d):
    return ((a // 2 + d) % 4) * 2 + a % 2


def y_by_core(a, b, c):
    y = (c // 2) * 2 + a % 2
    y = (y + (1 if c % 2 == 0 else -1)) % 4
    return (a // 2) * 2 + y % 2, b, (y // 2) * 2 + c % 2


ROUTES = {
    "x+": route(lambda a, b, c: (shift_x(a, 1), b, c)),
    "x-": route(lambda a, b, c: (shift_x(a, -1), b, c)),
    "x2": route(lambda a, b, c: (shift_x(a, 2), b, c)),
    "y": route(y_by_core),
    "y_lo": route(lambda a, b, c: (a ^ 1, b, c)),
    "y_hi": route(lambda a, b, c: (a, b, c ^ 2)),
    "z+": route(lambda a, b, c: (a, (b + 1) % 8, c)),
    "z-": route(lambda a, b, c: (a, (b - 1) % 8, c)),
    "core": route(lambda a, b, c: (a, b, c ^ 1)),
    "turn": route(lambda a, b, c: (b, a, c)),
}


def send(value, way):
    return lax.ppermute(value, AXES, ROUTES[way])


def split(value):
    high = value.astype(bf16)
    low = (value - high.astype(f32)).astype(bf16)
    return high, low


def dot3(left, right, dims):
    def one(l, r):
        return lax.dot_general(l, r, (dims, ((), ())), preferred_element_type=f32)

    return one(left[0], right[0]) + (one(left[0], right[1]) + one(left[1], right[0]))


def present(domains, orbital, block, fit):
    return domains[(orbital * NVB + block) * NPB + fit]


SMEM = pl.BlockSpec(memory_space=pltpu.SMEM)
VMEM = pl.BlockSpec(memory_space=pltpu.VMEM)


def params(mib, grid=0):
    order = {"dimension_semantics": ("arbitrary",) * grid} if grid else {}
    return pltpu.CompilerParams(vmem_limit_bytes=mib * 1024 * 1024, **order)


def cost(flops, mib):
    return pl.CostEstimate(flops=flops, bytes_accessed=mib * 1024 * 1024, transcendentals=0)


def block_rows(slot):
    return pl.ds(pl.multiple_of(slot * BLK, BLK), BLK)


def load(x, fit, orbital):
    return x[pl.ds(fit * BLK * O + orbital, BLK, stride=O), :]


def pack(target, x, domains, orbital, block):
    slot = jnp.int32(0)
    for fit in range(NPB):
        here = present(domains, orbital, block, fit)

        @pl.when(here == 1)
        def _(slot=slot, fit=fit):
            target[block_rows(slot), :] = load(x, fit, orbital)

        slot = slot + here


def pick_column(meta, domains, factors):
    def kernel(meta, domains, x, column):
        pack(column, x, domains, meta[1], 2 * meta[0] + lax.rem(meta[2], 2))

    return pl.pallas_call(
        kernel,
        out_shape=jax.ShapeDtypeStruct((PRES, BLK), f32),
        grid_spec=pltpu.PrefetchScalarGridSpec(
            num_scalar_prefetch=2,
            grid=(1,),
            in_specs=[pl.BlockSpec((NAUX * O, BLK), lambda n, meta, domains: (0, lax.rem(meta[2], 2)))],
            out_specs=pl.BlockSpec((PRES, BLK), lambda n, meta, domains: (0, 0)),
        ),
        compiler_params=params(56, 1),
        cost_estimate=cost(0, 5),
        name="pick_column",
    )(meta, domains, factors)


def prepare(meta, domains, factors):
    def kernel(meta, domains, x, rows_high, rows_low, piece, packed):
        a, z, c = meta[0], meta[1], meta[2]
        core = lax.rem(c, 2)
        for h in range(2):

            @pl.when(pl.program_id(0) == h)
            def _(h=h):
                lanes = slice(h * BLK, (h + 1) * BLK)
                for e in range(2):
                    store = packed.at[2 * e + h]
                    pack(store, x, domains, 2 * c + e, 2 * a + h)
                for r in range(4):
                    orbital = 2 * c + r if r < 2 else 2 * (c + 1 - 2 * core) + r - 2
                    for fit in range(NPB):
                        here = present(domains, orbital, 2 * a + h, fit).astype(f32)
                        high, low = split(load(x, fit, orbital) * here)
                        place = (slice(fit * BLK, (fit + 1) * BLK), slice(r * TILE + h * BLK, r * TILE + (h + 1) * BLK))
                        rows_high[place] = high
                        rows_low[place] = low
                window = pl.ds(pl.multiple_of(z * PIECE, 8), PIECE)
                for e in range(2):
                    piece[e, :, lanes] = packed[2 * e + h, window, :]

    return pl.pallas_call(
        kernel,
        out_shape=(
            jax.ShapeDtypeStruct((NAUX, 4 * TILE), bf16),
            jax.ShapeDtypeStruct((NAUX, 4 * TILE), bf16),
            jax.ShapeDtypeStruct((2, PIECE, TILE), f32),
        ),
        grid_spec=pltpu.PrefetchScalarGridSpec(
            num_scalar_prefetch=2,
            grid=(2,),
            in_specs=[pl.BlockSpec((NAUX * O, BLK), lambda n, meta, domains: (0, n))],
            out_specs=(
                pl.BlockSpec((NAUX, 4 * TILE), lambda n, meta, domains: (0, 0)),
                pl.BlockSpec((NAUX, 4 * TILE), lambda n, meta, domains: (0, 0)),
                pl.BlockSpec((2, PIECE, TILE), lambda n, meta, domains: (0, 0, 0)),
            ),
            scratch_shapes=[pltpu.VMEM((4, PRES, BLK), f32)],
        ),
        compiler_params=params(26, 1),
        cost_estimate=cost(0, 14),
        name="prepare",
    )(meta, domains, factors)


def tile_at(a, step):
    offset, flip = step
    return jnp.bitwise_xor(lax.rem(a + offset, 8), flip)


def dress(meta, domains, rows, row_energy, column_energy, blocks, steps, total, chunks, last):
    count = len(blocks)
    width = count * BLK
    has_total = total is not None

    def kernel(*refs):
        meta, domains, rows_high, rows_low, row_energy, column_energy = refs[:6]
        columns = refs[6 : 6 + count]
        refs = refs[6 + count :]
        before = None
        if has_total:
            before, refs = refs[0], refs[1:]
        out, wide, turned_high, turned_low = refs[:4]
        a, z, c = meta[0], meta[1], meta[2]
        core = lax.rem(c, 2)
        for q in range(count):
            slot = jnp.int32(0)
            span = slice(q * BLK, (q + 1) * BLK)
            for fit in range(NPB):
                here = present(domains, z, 2 * tile_at(a, steps[q]) + core, fit)
                block = columns[q][block_rows(jnp.minimum(slot, SLOTS - 1)), :]
                block = jnp.where(here == 1, block, 0.0)
                one, two = split(block)
                own = slice(fit * BLK, (fit + 1) * BLK)
                wide[own, q * BLK : (q + 1) * BLK] = one
                wide[own, width + q * BLK : width + (q + 1) * BLK] = one
                wide[own, 2 * width + q * BLK : 2 * width + (q + 1) * BLK] = two
                one, two = split(block.T)
                turned_high[span, own] = one
                turned_low[span, own] = two
                slot = slot + here
        for n, r in enumerate(chunks):
            span = slice(r * TILE, (r + 1) * TILE)
            direct = dot3(
                (turned_high[...], turned_low[...]), (rows_high[:, span], rows_low[:, span]), ((1,), (0,))
            )
            amps = -direct / (column_energy[...] + row_energy[:, span])
            high, low = split(amps)
            found = lax.dot_general(
                wide[...],
                jnp.concatenate([high, low, high], axis=0),
                (((1,), (0,)), ((), ())),
                preferred_element_type=f32,
            )
            if has_total:
                found = found + before[:, span]
            if not last:
                out[:, span] = found
                continue
            dense = refs[4].at[n]
            dense[...] = found
            orbital = 2 * c + r if r < 2 else 2 * (c + 1 - 2 * core) + r - 2
            for half in range(2):
                lanes = slice(half * BLK, (half + 1) * BLK)
                fits = [jnp.int32(0)] * SLOTS
                slot = jnp.int32(0)
                for fit in range(NPB):
                    here = present(domains, orbital, 2 * a + half, fit)
                    for s in range(SLOTS):
                        fits[s] = jnp.where((here == 1) & (slot == s), fit, fits[s])
                    slot = slot + here
                for k in range(24):
                    o = lax.rem(k // 3 + 8 - z, 8)
                    source = pl.ds(pl.multiple_of(fits[k // 4] * BLK + (k % 4) * 32, 32), 32)
                    out[o, n, (k % 3) * 32 : (k % 3 + 1) * 32, lanes] = dense[source, lanes]

    scratch = [
        pltpu.VMEM((NAUX, 3 * width), bf16),
        pltpu.VMEM((width, NAUX), bf16),
        pltpu.VMEM((width, NAUX), bf16),
    ]
    if last:
        out_shape = jax.ShapeDtypeStruct((8, len(chunks), PIECE, TILE), f32)
        scratch.append(pltpu.VMEM((len(chunks), NAUX, TILE), f32))
    else:
        out_shape = jax.ShapeDtypeStruct((NAUX, 4 * TILE), f32)
    operands = [meta, domains, *rows, row_energy, column_energy, *blocks]
    in_specs = [SMEM] * 2 + [VMEM] * (4 + count)
    if has_total:
        operands.append(total)
        in_specs.append(VMEM)
    return pl.pallas_call(
        kernel,
        out_shape=out_shape,
        in_specs=in_specs,
        out_specs=VMEM,
        scratch_shapes=scratch,
        compiler_params=params(20),
        cost_estimate=cost(12 * NAUX * width * len(chunks) * TILE, 14),
        name="dress",
    )(*operands)


def blocks_of(store, domains, orbital, first_block, put):
    for half in range(2):
        slot = jnp.int32(0)
        lanes = slice(half * BLK, (half + 1) * BLK)
        for fit in range(NPB):
            here = present(domains, orbital, first_block + half, fit)
            block = store[block_rows(jnp.minimum(slot, SLOTS - 1)), lanes]
            put(half, fit, jnp.where(here == 1, block, 0.0))
            slot = slot + here


def spread_far(meta, domains, pieces):
    def kernel(meta, domains, pieces, far_high, far_low, packed):
        z, c = meta[1], meta[2]
        for f in range(2):
            for p in range(8):
                packed[f, p * PIECE : (p + 1) * PIECE, :] = pieces[p, f]

            def put(half, fit, block, f=f):
                own = slice(fit * BLK, (fit + 1) * BLK)
                lanes = slice(f * TILE + half * BLK, f * TILE + (half + 1) * BLK)
                far_high[own, lanes], far_low[own, lanes] = split(block)

            blocks_of(packed.at[f], domains, 2 * c + f, 2 * z, put)

    shape = jax.ShapeDtypeStruct((NAUX, 2 * TILE), bf16)
    return pl.pallas_call(
        kernel,
        out_shape=(shape, shape),
        in_specs=[SMEM, SMEM, VMEM],
        out_specs=(VMEM, VMEM),
        scratch_shapes=[pltpu.VMEM((2, PRES, TILE), f32)],
        compiler_params=params(56),
        cost_estimate=cost(0, 4),
        name="spread_far",
    )(meta, domains, pieces)


def finish(meta, domains, occ_energy, vir_near, col_energy, far, near, groups, filled):
    near_parts, near_arrays = near
    n_near = len(near_arrays)
    has_filled = filled is not None

    def kernel(*refs):
        meta, domains, occ, vir_near, col_energy, far_high, far_low = refs[:7]
        near_refs = refs[7 : 7 + n_near]
        out, packed, high, low = refs[7 + n_near + (1 if has_filled else 0) :]
        a, z, c = meta[0], meta[1], meta[2]
        step = pl.program_id(0)
        upper, e = step // 2, lax.rem(step, 2)

        def rows_of(place):
            return pl.ds(pl.multiple_of(place * PIECE, 8), PIECE)

        orbital = 2 * jnp.bitwise_xor(c, groups[0] + upper * (groups[1] - groups[0])) + e
        for offset, which, part in near_parts:
            place = rows_of(lax.rem(z + offset, 8))
            if part is not None:
                packed[place, :] = near_refs[which][part + (upper, e)]
                continue
            for n, (w, p) in enumerate(which):

                @pl.when(upper == n)
                def _(w=w, p=p, place=place):
                    packed[place, :] = near_refs[w][p + (e,)]

        def put(half, fit, block):
            own = slice(fit * BLK, (fit + 1) * BLK)
            span = slice(half * BLK, (half + 1) * BLK)
            high[span, own], low[span, own] = split(block.T)

        blocks_of(packed, domains, orbital, 2 * a, put)
        residual = dot3((high[...], low[...]), (far_high[...], far_low[...]), ((1,), (0,)))
        energy = (vir_near[...] - occ[orbital]) + col_energy[...]
        result = (residual * (-SCALE)) / energy
        for j in range(2):
            for b in range(2):
                lanes = slice(j * TILE + b * BLK, j * TILE + (b + 1) * BLK)
                out[pl.ds(2 * b + j, TILE, stride=4), :] = result[:, lanes]

    def place(n, meta, domains, occ):
        pair = jnp.bitwise_xor(meta[2], groups[0] + (n // 2) * (groups[1] - groups[0]))
        return 2 * pair + lax.rem(n, 2), 0

    operands = [meta, domains, occ_energy, vir_near, col_energy, *far, *near_arrays]
    in_specs = [VMEM] * (4 + n_near)
    aliases = {}
    if has_filled:
        aliases = {len(operands): 0}
        operands.append(filled)
        in_specs.append(pl.BlockSpec(memory_space=pl.ANY))
    return pl.pallas_call(
        kernel,
        out_shape=jax.ShapeDtypeStruct((O * TILE * 4, BLK), f32),
        grid_spec=pltpu.PrefetchScalarGridSpec(
            num_scalar_prefetch=3,
            grid=(4,),
            in_specs=in_specs,
            out_specs=pl.BlockSpec((TILE * 4, BLK), place),
            scratch_shapes=[
                pltpu.VMEM((PRES, TILE), f32),
                pltpu.VMEM((TILE, NAUX), bf16),
                pltpu.VMEM((TILE, NAUX), bf16),
            ],
        ),
        input_output_aliases=aliases,
        compiler_params=params(56, 1),
        cost_estimate=cost(6 * NAUX * 1024 * 512, 8),
        name="finish",
    )(*operands)


def body(factors, domains, occ_energy, vir_energy):
    a = lax.axis_index("va")
    z = lax.axis_index("vb")
    c = lax.axis_index("aux")
    core = c % 2
    meta = jnp.stack([a, z, c]).astype(jnp.int32)
    flags = domains.reshape(-1)
    flat = factors.reshape(NAUX * O, TILE)

    column = pick_column(meta, flags, flat)
    right, left = send(column, "x+"), send(column, "x-")
    y_own, y_right, y_left = (send(block, "y") for block in (column, right, left))
    rows_high, rows_low, piece = prepare(meta, flags, flat)
    rows = (rows_high, rows_low)
    beyond = send(lax.optimization_barrier((column, right, left, piece))[0], "x2")
    vir_near = lax.dynamic_slice_in_dim(vir_energy, a * TILE, TILE)
    occ_pairs = occ_energy.reshape(4, 2)
    occ_rows = jnp.concatenate([occ_pairs[c], occ_pairs[c ^ 1]])
    row_energy = (vir_near[None, :] - occ_rows[:, None]).reshape(1, 4 * TILE)
    tiles = jnp.stack([(a + d) % 8 ^ f for d, f in ((0, 0), (0, 1), (6, 0), (2, 0), (6, 1), (2, 1), (4, 0), (4, 1))])
    energies = (vir_energy.reshape(8, 2, BLK)[:, core][tiles] - occ_energy[z]).reshape(8 * BLK, 1)

    def add(n, blocks, steps, total, chunks=(0, 1, 2, 3), last=False):
        part = energies[2 * n * BLK : 2 * (n + 1) * BLK]
        return dress(meta, flags, rows, row_energy, part, blocks, steps, total, chunks, last)

    total = add(0, [column, y_own], [(0, 0), (0, 1)], None)
    ready, total = lax.optimization_barrier((beyond, total))
    y_beyond = send(ready, "y")
    total = add(1, [right, left], [(6, 0), (2, 0)], total)
    total = add(2, [y_right, y_left], [(6, 1), (2, 1)], total)
    final = ([beyond, y_beyond], [(4, 0), (4, 1)], total)
    give = add(3, *final, chunks=(2, 3), last=True)

    first = send(give[3:5], "core")
    rest = send(jnp.concatenate([give[:3], give[5:]]), "core")
    keep = add(3, *final, chunks=(0, 1), last=True)
    got = [rest[0], rest[1], rest[2], first[0], first[1], rest[3], rest[4], rest[5]]
    plus = send(keep[3] + got[3], "z+")
    minus = send(keep[4] + got[4], "z-")
    minus = send(keep[5] + got[5] + minus, "z-")
    plus = send(keep[2] + got[2] + plus, "z+")
    minus = send(keep[6] + got[6] + minus, "z-")
    plus = send(keep[1] + got[1] + plus, "z+")
    minus = send(keep[7] + got[7] + minus, "z-")
    summed = (keep[0] + got[0]) + (plus + minus)
    combined = piece + 2.0 * summed

    turned = send(combined, "turn")
    across = send(combined, "y_hi")
    combined, turned, across = lax.optimization_barrier((combined, turned, across))
    far = spread_far(meta, flags, lax.all_gather(turned, "va"))

    both = jnp.stack([combined, across])
    plus1, minus1 = send(both, "z+"), send(both, "z-")
    plus2, minus2 = send(plus1, "z+"), send(minus1, "z-")
    plus3, minus3 = send(plus2, "z+"), send(minus2, "z-")
    early = send(jnp.stack([both, plus1, minus1, plus2, minus2]), "core")
    plus4, minus4 = send(plus3[0], "z+"), send(minus3[1], "z-")
    late = send(jnp.stack([plus3, minus3, jnp.stack([plus4, minus4])]), "core")
    ring = [both, plus1, minus1, plus2, minus2, plus3, minus3, plus4, minus4]
    offsets = [0, 7, 1, 6, 2, 5, 3]
    ring_parts = [(o, n, ()) for n, o in enumerate(offsets)] + [(4, ((7, ()), (8, ())), None)]
    swap_parts = [(o, 0, (n,)) if n < 5 else (o, 1, (n - 5,)) for n, o in enumerate(offsets)] + [(4, 1, (2,))]
    pair_energy = lax.dynamic_slice_in_dim(vir_energy, z * TILE, TILE)[None, :] - occ_pairs[c][:, None]

    def rows_for(near, groups, filled):
        return finish(
            meta,
            flags,
            occ_energy,
            vir_near.reshape(TILE, 1),
            pair_energy.reshape(1, 2 * TILE),
            far,
            near,
            groups,
            filled,
        )

    filled = rows_for((ring_parts, ring), (0, 2), None)
    filled = rows_for((swap_parts, [early, late]), (1, 3), filled)
    return filled.reshape(O, TILE, 2, 2, BLK).transpose(0, 1, 3, 2, 4).reshape(O, TILE, 2, TILE)


def solution(mesh):
    placed = (P(None, None, "va"), P(), P(), P())
    return jax.shard_map(
        body, mesh=mesh, in_specs=placed, out_specs=P(None, "va", "aux", "vb"), check_vma=False
    )
```

```python
import math

import jax
import jax.numpy as jnp
from jax import lax
from jax.experimental import pallas as pl
from jax.experimental.pallas import tpu as pltpu
from jax.sharding import PartitionSpec as P

O = 8
V = 2048
NAUX = 1024
BLK = 128
NPB = 8
NVB = 16
SLOTS = 6
PRES = SLOTS * BLK
PIECE = PRES // 8
TILE = 256
SCALE = 8.0 * O * V / math.sqrt(NAUX)
AXES = ("va", "vb", "aux")
f32 = jnp.float32
bf16 = jnp.bfloat16


def route(move):
    pairs = []
    for a in range(8):
        for b in range(8):
            for c in range(4):
                A, B, C = move(a, b, c)
                pairs.append(((a * 8 + b) * 4 + c, (A * 8 + B) * 4 + C))
    return pairs


def shift_x(a, d):
    return ((a // 2 + d) % 4) * 2 + a % 2


def y_by_core(a, b, c):
    y = (c // 2) * 2 + a % 2
    y = (y + (1 if c % 2 == 0 else -1)) % 4
    return (a // 2) * 2 + y % 2, b, (y // 2) * 2 + c % 2


ROUTES = {
    "x+": route(lambda a, b, c: (shift_x(a, 1), b, c)),
    "x-": route(lambda a, b, c: (shift_x(a, -1), b, c)),
    "x2": route(lambda a, b, c: (shift_x(a, 2), b, c)),
    "y": route(y_by_core),
    "y_lo": route(lambda a, b, c: (a ^ 1, b, c)),
    "y_hi": route(lambda a, b, c: (a, b, c ^ 2)),
    "z+": route(lambda a, b, c: (a, (b + 1) % 8, c)),
    "z-": route(lambda a, b, c: (a, (b - 1) % 8, c)),
    "x_by_core": route(lambda a, b, c: (shift_x(a, 1 - 2 * (c % 2)), b, c)),
    "core": route(lambda a, b, c: (a, b, c ^ 1)),
    "turn": route(lambda a, b, c: (b, a, c)),
}


def send(value, way):
    return lax.ppermute(value, AXES, ROUTES[way])


def split(value):
    high = value.astype(bf16)
    low = (value - high.astype(f32)).astype(bf16)
    return high, low


def dot3(left, right, dims):
    def one(l, r):
        return lax.dot_general(l, r, (dims, ((), ())), preferred_element_type=f32)

    return one(left[0], right[0]) + (one(left[0], right[1]) + one(left[1], right[0]))


def present(domains, orbital, block, fit):
    return domains[(orbital * NVB + block) * NPB + fit]


SMEM = pl.BlockSpec(memory_space=pltpu.SMEM)
VMEM = pl.BlockSpec(memory_space=pltpu.VMEM)


def params(mib, grid=0):
    order = {"dimension_semantics": ("arbitrary",) * grid} if grid else {}
    return pltpu.CompilerParams(vmem_limit_bytes=mib * 1024 * 1024, **order)


def cost(flops, mib):
    return pl.CostEstimate(flops=flops, bytes_accessed=mib * 1024 * 1024, transcendentals=0)


def block_rows(slot):
    return pl.ds(pl.multiple_of(slot * BLK, BLK), BLK)


def load(x, fit, orbital):
    return x[pl.ds(fit * BLK * O + orbital, BLK, stride=O), :]


def pack(target, x, domains, orbital, block):
    slot = jnp.int32(0)
    for fit in range(NPB):
        here = present(domains, orbital, block, fit)

        @pl.when(here == 1)
        def _(slot=slot, fit=fit):
            target[block_rows(slot), :] = load(x, fit, orbital)

        slot = slot + here


def pick_column(meta, domains, factors):
    def kernel(meta, domains, x, column):
        pack(column, x, domains, meta[1], 2 * meta[0] + lax.rem(meta[2], 2))

    return pl.pallas_call(
        kernel,
        out_shape=jax.ShapeDtypeStruct((PRES, BLK), f32),
        grid_spec=pltpu.PrefetchScalarGridSpec(
            num_scalar_prefetch=2,
            grid=(1,),
            in_specs=[pl.BlockSpec((NAUX * O, BLK), lambda n, meta, domains: (0, lax.rem(meta[2], 2)))],
            out_specs=pl.BlockSpec((PRES, BLK), lambda n, meta, domains: (0, 0)),
        ),
        compiler_params=params(56, 1),
        cost_estimate=cost(0, 5),
        name="pick_column",
    )(meta, domains, factors)


def prepare(meta, domains, factors):
    def kernel(meta, domains, x, rows_high, rows_low, piece, packed):
        a, z, c = meta[0], meta[1], meta[2]
        core = lax.rem(c, 2)
        for h in range(2):

            @pl.when(pl.program_id(0) == h)
            def _(h=h):
                lanes = slice(h * BLK, (h + 1) * BLK)
                for e in range(2):
                    store = packed.at[2 * e + h]
                    pack(store, x, domains, 2 * c + e, 2 * a + h)
                for r in range(4):
                    orbital = 2 * c + r if r < 2 else 2 * (c + 1 - 2 * core) + r - 2
                    for fit in range(NPB):
                        here = present(domains, orbital, 2 * a + h, fit).astype(f32)
                        high, low = split(load(x, fit, orbital) * here)
                        place = (slice(fit * BLK, (fit + 1) * BLK), slice(r * TILE + h * BLK, r * TILE + (h + 1) * BLK))
                        rows_high[place] = high
                        rows_low[place] = low
                window = pl.ds(pl.multiple_of(z * PIECE, 8), PIECE)
                for e in range(2):
                    piece[e, :, lanes] = packed[2 * e + h, window, :]

    return pl.pallas_call(
        kernel,
        out_shape=(
            jax.ShapeDtypeStruct((NAUX, 4 * TILE), bf16),
            jax.ShapeDtypeStruct((NAUX, 4 * TILE), bf16),
            jax.ShapeDtypeStruct((2, PIECE, TILE), f32),
        ),
        grid_spec=pltpu.PrefetchScalarGridSpec(
            num_scalar_prefetch=2,
            grid=(2,),
            in_specs=[pl.BlockSpec((NAUX * O, BLK), lambda n, meta, domains: (0, n))],
            out_specs=(
                pl.BlockSpec((NAUX, 4 * TILE), lambda n, meta, domains: (0, 0)),
                pl.BlockSpec((NAUX, 4 * TILE), lambda n, meta, domains: (0, 0)),
                pl.BlockSpec((2, PIECE, TILE), lambda n, meta, domains: (0, 0, 0)),
            ),
            scratch_shapes=[pltpu.VMEM((4, PRES, BLK), f32)],
        ),
        compiler_params=params(26, 1),
        cost_estimate=cost(0, 14),
        name="prepare",
    )(meta, domains, factors)


def tile_at(a, step):
    offset, flip = step
    return jnp.bitwise_xor(lax.rem(a + offset, 8), flip)


def dress(meta, domains, rows, row_energy, column_energy, blocks, steps, total, chunks, last):
    count = len(blocks)
    width = count * BLK
    has_total = total is not None

    def kernel(*refs):
        meta, domains, rows_high, rows_low, row_energy, column_energy = refs[:6]
        columns = refs[6 : 6 + count]
        refs = refs[6 + count :]
        before = None
        if has_total:
            before, refs = refs[0], refs[1:]
        out, wide, turned_high, turned_low = refs[:4]
        a, z, c = meta[0], meta[1], meta[2]
        core = lax.rem(c, 2)
        for q in range(count):
            slot = jnp.int32(0)
            span = slice(q * BLK, (q + 1) * BLK)
            for fit in range(NPB):
                here = present(domains, z, 2 * tile_at(a, steps[q]) + core, fit)
                block = columns[q][block_rows(jnp.minimum(slot, SLOTS - 1)), :]
                block = jnp.where(here == 1, block, 0.0)
                one, two = split(block)
                own = slice(fit * BLK, (fit + 1) * BLK)
                wide[own, q * BLK : (q + 1) * BLK] = one
                wide[own, width + q * BLK : width + (q + 1) * BLK] = one
                wide[own, 2 * width + q * BLK : 2 * width + (q + 1) * BLK] = two
                one, two = split(block.T)
                turned_high[span, own] = one
                turned_low[span, own] = two
                slot = slot + here
        for n, r in enumerate(chunks):
            span = slice(r * TILE, (r + 1) * TILE)
            direct = dot3(
                (turned_high[...], turned_low[...]), (rows_high[:, span], rows_low[:, span]), ((1,), (0,))
            )
            amps = -direct / (column_energy[...] + row_energy[:, span])
            high, low = split(amps)
            found = lax.dot_general(
                wide[...],
                jnp.concatenate([high, low, high], axis=0),
                (((1,), (0,)), ((), ())),
                preferred_element_type=f32,
            )
            if has_total:
                found = found + before[:, span]
            if not last:
                out[:, span] = found
                continue
            dense = refs[4].at[n]
            dense[...] = found
            orbital = 2 * c + r if r < 2 else 2 * (c + 1 - 2 * core) + r - 2
            for half in range(2):
                lanes = slice(half * BLK, (half + 1) * BLK)
                fits = [jnp.int32(0)] * SLOTS
                slot = jnp.int32(0)
                for fit in range(NPB):
                    here = present(domains, orbital, 2 * a + half, fit)
                    for s in range(SLOTS):
                        fits[s] = jnp.where((here == 1) & (slot == s), fit, fits[s])
                    slot = slot + here
                for k in range(24):
                    o = lax.rem(k // 3 + 8 - z, 8)
                    source = pl.ds(pl.multiple_of(fits[k // 4] * BLK + (k % 4) * 32, 32), 32)
                    out[o, n, (k % 3) * 32 : (k % 3 + 1) * 32, lanes] = dense[source, lanes]

    scratch = [
        pltpu.VMEM((NAUX, 3 * width), bf16),
        pltpu.VMEM((width, NAUX), bf16),
        pltpu.VMEM((width, NAUX), bf16),
    ]
    if last:
        out_shape = jax.ShapeDtypeStruct((8, len(chunks), PIECE, TILE), f32)
        scratch.append(pltpu.VMEM((len(chunks), NAUX, TILE), f32))
    else:
        out_shape = jax.ShapeDtypeStruct((NAUX, 4 * TILE), f32)
    operands = [meta, domains, *rows, row_energy, column_energy, *blocks]
    in_specs = [SMEM] * 2 + [VMEM] * (4 + count)
    if has_total:
        operands.append(total)
        in_specs.append(VMEM)
    return pl.pallas_call(
        kernel,
        out_shape=out_shape,
        in_specs=in_specs,
        out_specs=VMEM,
        scratch_shapes=scratch,
        compiler_params=params(20),
        cost_estimate=cost(12 * NAUX * width * len(chunks) * TILE, 14),
        name="dress",
    )(*operands)


def blocks_of(store, domains, orbital, first_block, put):
    for half in range(2):
        slot = jnp.int32(0)
        lanes = slice(half * BLK, (half + 1) * BLK)
        for fit in range(NPB):
            here = present(domains, orbital, first_block + half, fit)
            block = store[block_rows(jnp.minimum(slot, SLOTS - 1)), lanes]
            put(half, fit, jnp.where(here == 1, block, 0.0))
            slot = slot + here


def pass_on(value, after):
    def kernel(value, after, out):
        out[...] = value[...]

    return pl.pallas_call(
        kernel,
        out_shape=jax.ShapeDtypeStruct(value.shape, value.dtype),
        in_specs=[VMEM, pl.BlockSpec(memory_space=pl.ANY)],
        out_specs=VMEM,
        compiler_params=params(4),
        cost_estimate=cost(0, 1),
        name="pass_on",
    )(value, after)


def spread_far(meta, domains, arrays, parts):
    def kernel(meta, domains, *refs):
        arrays, (far_high, far_low, packed) = refs[:4], refs[4:]
        a, z, c = meta[0], meta[1], meta[2]
        for f in range(2):
            for where, which, part in parts:
                place = pl.ds(pl.multiple_of(tile_at(a, where) * PIECE, 8), PIECE)
                packed.at[f][place, :] = arrays[which][part, f]

            def put(half, fit, block, f=f):
                own = slice(fit * BLK, (fit + 1) * BLK)
                lanes = slice(f * TILE + half * BLK, f * TILE + (half + 1) * BLK)
                far_high[own, lanes], far_low[own, lanes] = split(block)

            blocks_of(packed.at[f], domains, 2 * c + f, 2 * z, put)

    shape = jax.ShapeDtypeStruct((NAUX, 2 * TILE), bf16)
    return pl.pallas_call(
        kernel,
        out_shape=(shape, shape),
        in_specs=[SMEM, SMEM] + [VMEM] * 4,
        out_specs=(VMEM, VMEM),
        scratch_shapes=[pltpu.VMEM((2, PRES, TILE), f32)],
        compiler_params=params(56),
        cost_estimate=cost(0, 4),
        name="spread_far",
    )(meta, domains, *arrays)


def finish(meta, domains, occ_energy, vir_near, col_energy, far, near, groups, filled):
    near_parts, near_arrays = near
    n_near = len(near_arrays)
    has_filled = filled is not None

    def kernel(*refs):
        meta, domains, occ, vir_near, col_energy, far_high, far_low = refs[:7]
        near_refs = refs[7 : 7 + n_near]
        out, packed, high, low = refs[7 + n_near + (1 if has_filled else 0) :]
        a, z, c = meta[0], meta[1], meta[2]
        step = pl.program_id(0)
        upper, e = step // 2, lax.rem(step, 2)

        def rows_of(place):
            return pl.ds(pl.multiple_of(place * PIECE, 8), PIECE)

        orbital = 2 * jnp.bitwise_xor(c, groups[0] + upper * (groups[1] - groups[0])) + e
        for offset, which, part in near_parts:
            place = rows_of(lax.rem(z + offset, 8))
            if part is not None:
                packed[place, :] = near_refs[which][part + (upper, e)]
                continue
            for n, (w, p) in enumerate(which):

                @pl.when(upper == n)
                def _(w=w, p=p, place=place):
                    packed[place, :] = near_refs[w][p + (e,)]

        def put(half, fit, block):
            own = slice(fit * BLK, (fit + 1) * BLK)
            span = slice(half * BLK, (half + 1) * BLK)
            high[span, own], low[span, own] = split(block.T)

        blocks_of(packed, domains, orbital, 2 * a, put)
        residual = dot3((high[...], low[...]), (far_high[...], far_low[...]), ((1,), (0,)))
        energy = (vir_near[...] - occ[orbital]) + col_energy[...]
        result = (residual * (-SCALE)) / energy
        for j in range(2):
            for b in range(2):
                lanes = slice(j * TILE + b * BLK, j * TILE + (b + 1) * BLK)
                out[pl.ds(2 * b + j, TILE, stride=4), :] = result[:, lanes]

    def place(n, meta, domains, occ):
        pair = jnp.bitwise_xor(meta[2], groups[0] + (n // 2) * (groups[1] - groups[0]))
        return 2 * pair + lax.rem(n, 2), 0

    operands = [meta, domains, occ_energy, vir_near, col_energy, *far, *near_arrays]
    in_specs = [VMEM] * (4 + n_near)
    aliases = {}
    if has_filled:
        aliases = {len(operands): 0}
        operands.append(filled)
        in_specs.append(pl.BlockSpec(memory_space=pl.ANY))
    return pl.pallas_call(
        kernel,
        out_shape=jax.ShapeDtypeStruct((O * TILE * 4, BLK), f32),
        grid_spec=pltpu.PrefetchScalarGridSpec(
            num_scalar_prefetch=3,
            grid=(4,),
            in_specs=in_specs,
            out_specs=pl.BlockSpec((TILE * 4, BLK), place),
            scratch_shapes=[
                pltpu.VMEM((PRES, TILE), f32),
                pltpu.VMEM((TILE, NAUX), bf16),
                pltpu.VMEM((TILE, NAUX), bf16),
            ],
        ),
        input_output_aliases=aliases,
        compiler_params=params(56, 1),
        cost_estimate=cost(6 * NAUX * 1024 * 512, 8),
        name="finish",
    )(*operands)


def body(factors, domains, occ_energy, vir_energy):
    a = lax.axis_index("va")
    z = lax.axis_index("vb")
    c = lax.axis_index("aux")
    core = c % 2
    meta = jnp.stack([a, z, c]).astype(jnp.int32)
    flags = domains.reshape(-1)
    flat = factors.reshape(NAUX * O, TILE)

    column = pick_column(meta, flags, flat)
    right, left, y_own = send(column, "x+"), send(column, "x-"), send(column, "y")
    rows_high, rows_low, piece = prepare(meta, flags, flat)
    rows = (rows_high, rows_low)
    piece, near_right, near_left = lax.optimization_barrier((piece, right, left))
    beyond = send(jnp.where(core == 0, near_right, near_left), "x_by_core")
    y_right, y_left, y_beyond = (send(block, "y") for block in (near_right, near_left, beyond))
    vir_near = lax.dynamic_slice_in_dim(vir_energy, a * TILE, TILE)
    occ_pairs = occ_energy.reshape(4, 2)
    occ_rows = jnp.concatenate([occ_pairs[c], occ_pairs[c ^ 1]])
    row_energy = (vir_near[None, :] - occ_rows[:, None]).reshape(1, 4 * TILE)
    tiles = jnp.stack([(a + d) % 8 ^ f for d, f in ((0, 0), (0, 1), (6, 0), (2, 0), (6, 1), (2, 1), (4, 0), (4, 1))])
    energies = (vir_energy.reshape(8, 2, BLK)[:, core][tiles] - occ_energy[z]).reshape(8 * BLK, 1)

    def add(n, blocks, steps, total, chunks=(0, 1, 2, 3), last=False):
        part = energies[2 * n * BLK : 2 * (n + 1) * BLK]
        return dress(meta, flags, rows, row_energy, part, blocks, steps, total, chunks, last)

    total = add(0, [column, y_own], [(0, 0), (0, 1)], None)
    total = add(1, [right, left], [(6, 0), (2, 0)], total)
    total = add(2, [y_right, y_left], [(6, 1), (2, 1)], total)
    final = ([beyond, y_beyond], [(4, 0), (4, 1)], total)
    give = add(3, *final, chunks=(2, 3), last=True)

    first = send(give[3:5], "core")
    rest = send(jnp.concatenate([give[:3], give[5:]]), "core")
    keep = add(3, *final, chunks=(0, 1), last=True)
    got = [rest[0], rest[1], rest[2], first[0], first[1], rest[3], rest[4], rest[5]]
    plus = send(keep[3] + got[3], "z+")
    minus = send(keep[4] + got[4], "z-")
    minus = send(keep[5] + got[5] + minus, "z-")
    plus = send(keep[2] + got[2] + plus, "z+")
    minus = send(keep[6] + got[6] + minus, "z-")
    plus = send(keep[1] + got[1] + plus, "z+")
    minus = send(keep[7] + got[7] + minus, "z-")
    summed = (keep[0] + got[0]) + (plus + minus)
    combined = piece + 2.0 * summed

    both = jnp.stack([combined, send(combined, "y_hi")])
    plus1, minus1 = send(both, "z+"), send(both, "z-")
    turned = send(pass_on(combined, both), "turn")
    plus1, minus1, turned = lax.optimization_barrier((plus1, minus1, turned))
    plus2, minus2 = send(plus1, "z+"), send(minus1, "z-")
    far_pair = jnp.stack([turned, send(pass_on(turned, plus1), "y_lo")])
    plus2, minus2, far_pair = lax.optimization_barrier((plus2, minus2, far_pair))

    plus3, minus3 = send(plus2, "z+"), send(minus2, "z-")
    moved = pass_on(far_pair, plus2)
    far_right, far_left = send(moved, "x+"), send(moved, "x-")
    plus3, minus3, far_right, far_left = lax.optimization_barrier((plus3, minus3, far_right, far_left))
    far_beyond = send(pass_on(jnp.where(core == 0, far_right, far_left), plus3), "x_by_core")
    far_parts = []
    for which, offset in enumerate([0, 6, 2, 4]):
        far_parts += [((offset, 0), which, 0), ((offset, 1), which, 1)]
    far = spread_far(meta, flags, [far_pair, far_right, far_left, far_beyond], far_parts)
    early = send(jnp.stack([both, plus1, minus1, plus2, minus2]), "core")
    plus4, minus4 = send(plus3[0], "z+"), send(minus3[1], "z-")
    late = send(jnp.stack([plus3, minus3, jnp.stack([plus4, minus4])]), "core")
    ring = [both, plus1, minus1, plus2, minus2, plus3, minus3, plus4, minus4]
    offsets = [0, 7, 1, 6, 2, 5, 3]
    ring_parts = [(o, n, ()) for n, o in enumerate(offsets)] + [(4, ((7, ()), (8, ())), None)]
    swap_parts = [(o, 0, (n,)) if n < 5 else (o, 1, (n - 5,)) for n, o in enumerate(offsets)] + [(4, 1, (2,))]
    pair_energy = lax.dynamic_slice_in_dim(vir_energy, z * TILE, TILE)[None, :] - occ_pairs[c][:, None]

    def rows_for(near, groups, filled):
        return finish(
            meta,
            flags,
            occ_energy,
            vir_near.reshape(TILE, 1),
            pair_energy.reshape(1, 2 * TILE),
            far,
            near,
            groups,
            filled,
        )

    filled = rows_for((ring_parts, ring), (0, 2), None)
    filled = rows_for((swap_parts, [early, late]), (1, 3), filled)
    return filled.reshape(O, TILE, 2, 2, BLK).transpose(0, 1, 3, 2, 4).reshape(O, TILE, 2, TILE)


def solution(mesh):
    placed = (P(None, None, "va"), P(), P(), P())
    return jax.shard_map(
        body, mesh=mesh, in_specs=placed, out_specs=P(None, "va", "aux", "vb"), check_vma=False
    )
```

```python
import math

import jax
import jax.numpy as jnp
from jax import lax
from jax.experimental import pallas as pl
from jax.experimental.pallas import tpu as pltpu
from jax.sharding import PartitionSpec as P

O = 8
V = 2048
NAUX = 1024
BLK = 128
NPB = 8
NVB = 16
SLOTS = 6
PRES = SLOTS * BLK
PIECE = PRES // 8
TILE = 256
SCALE = 8.0 * O * V / math.sqrt(NAUX)
AXES = ("va", "vb", "aux")
f32 = jnp.float32
bf16 = jnp.bfloat16


def route(move):
    pairs = []
    for a in range(8):
        for b in range(8):
            for c in range(4):
                A, B, C = move(a, b, c)
                pairs.append(((a * 8 + b) * 4 + c, (A * 8 + B) * 4 + C))
    return pairs


def shift_x(a, d):
    return ((a // 2 + d) % 4) * 2 + a % 2


def y_by_core(a, b, c):
    y = (c // 2) * 2 + a % 2
    y = (y + (1 if c % 2 == 0 else -1)) % 4
    return (a // 2) * 2 + y % 2, b, (y // 2) * 2 + c % 2


ROUTES = {
    "x+": route(lambda a, b, c: (shift_x(a, 1), b, c)),
    "x-": route(lambda a, b, c: (shift_x(a, -1), b, c)),
    "x2": route(lambda a, b, c: (shift_x(a, 2), b, c)),
    "y": route(y_by_core),
    "y_lo": route(lambda a, b, c: (a ^ 1, b, c)),
    "y_hi": route(lambda a, b, c: (a, b, c ^ 2)),
    "z+": route(lambda a, b, c: (a, (b + 1) % 8, c)),
    "z-": route(lambda a, b, c: (a, (b - 1) % 8, c)),
    "x_by_core": route(lambda a, b, c: (shift_x(a, 1 - 2 * (c % 2)), b, c)),
    "core": route(lambda a, b, c: (a, b, c ^ 1)),
    "turn": route(lambda a, b, c: (b, a, c)),
}


def send(value, way):
    return lax.ppermute(value, AXES, ROUTES[way])


def split(value):
    high = value.astype(bf16)
    low = (value - high.astype(f32)).astype(bf16)
    return high, low


def dot3(left, right, dims):
    def one(l, r):
        return lax.dot_general(l, r, (dims, ((), ())), preferred_element_type=f32)

    return one(left[0], right[0]) + (one(left[0], right[1]) + one(left[1], right[0]))


def present(domains, orbital, block, fit):
    return domains[(orbital * NVB + block) * NPB + fit]


SMEM = pl.BlockSpec(memory_space=pltpu.SMEM)
VMEM = pl.BlockSpec(memory_space=pltpu.VMEM)


def params(mib, grid=0):
    order = {"dimension_semantics": ("arbitrary",) * grid} if grid else {}
    return pltpu.CompilerParams(vmem_limit_bytes=mib * 1024 * 1024, **order)


def cost(flops, mib):
    return pl.CostEstimate(flops=flops, bytes_accessed=mib * 1024 * 1024, transcendentals=0)


def block_rows(slot):
    return pl.ds(pl.multiple_of(slot * BLK, BLK), BLK)


def load(x, fit, orbital):
    return x[pl.ds(fit * BLK * O + orbital, BLK, stride=O), :]


def pack(target, x, domains, orbital, block):
    slot = jnp.int32(0)
    for fit in range(NPB):
        here = present(domains, orbital, block, fit)

        @pl.when(here == 1)
        def _(slot=slot, fit=fit):
            target[block_rows(slot), :] = load(x, fit, orbital)

        slot = slot + here


def pick_column(meta, domains, factors):
    def kernel(meta, domains, x, column):
        pack(column, x, domains, meta[1], 2 * meta[0] + lax.rem(meta[2], 2))

    return pl.pallas_call(
        kernel,
        out_shape=jax.ShapeDtypeStruct((PRES, BLK), f32),
        grid_spec=pltpu.PrefetchScalarGridSpec(
            num_scalar_prefetch=2,
            grid=(1,),
            in_specs=[pl.BlockSpec((NAUX * O, BLK), lambda n, meta, domains: (0, lax.rem(meta[2], 2)))],
            out_specs=pl.BlockSpec((PRES, BLK), lambda n, meta, domains: (0, 0)),
        ),
        compiler_params=params(56, 1),
        cost_estimate=cost(0, 5),
        name="pick_column",
    )(meta, domains, factors)


def prepare(meta, domains, factors):
    def kernel(meta, domains, x, rows_high, rows_low, piece, packed):
        a, z, c = meta[0], meta[1], meta[2]
        core = lax.rem(c, 2)
        for h in range(2):

            @pl.when(pl.program_id(0) == h)
            def _(h=h):
                lanes = slice(h * BLK, (h + 1) * BLK)
                for e in range(2):
                    store = packed.at[2 * e + h]
                    pack(store, x, domains, 2 * c + e, 2 * a + h)
                for r in range(4):
                    orbital = 2 * c + r if r < 2 else 2 * (c + 1 - 2 * core) + r - 2
                    for fit in range(NPB):
                        here = present(domains, orbital, 2 * a + h, fit).astype(f32)
                        high, low = split(load(x, fit, orbital) * here)
                        place = (slice(fit * BLK, (fit + 1) * BLK), slice(r * TILE + h * BLK, r * TILE + (h + 1) * BLK))
                        rows_high[place] = high
                        rows_low[place] = low
                window = pl.ds(pl.multiple_of(z * PIECE, 8), PIECE)
                for e in range(2):
                    piece[e, :, lanes] = packed[2 * e + h, window, :]

    return pl.pallas_call(
        kernel,
        out_shape=(
            jax.ShapeDtypeStruct((NAUX, 4 * TILE), bf16),
            jax.ShapeDtypeStruct((NAUX, 4 * TILE), bf16),
            jax.ShapeDtypeStruct((2, PIECE, TILE), f32),
        ),
        grid_spec=pltpu.PrefetchScalarGridSpec(
            num_scalar_prefetch=2,
            grid=(2,),
            in_specs=[pl.BlockSpec((NAUX * O, BLK), lambda n, meta, domains: (0, n))],
            out_specs=(
                pl.BlockSpec((NAUX, 4 * TILE), lambda n, meta, domains: (0, 0)),
                pl.BlockSpec((NAUX, 4 * TILE), lambda n, meta, domains: (0, 0)),
                pl.BlockSpec((2, PIECE, TILE), lambda n, meta, domains: (0, 0, 0)),
            ),
            scratch_shapes=[pltpu.VMEM((4, PRES, BLK), f32)],
        ),
        compiler_params=params(26, 1),
        cost_estimate=cost(0, 14),
        name="prepare",
    )(meta, domains, factors)


def tile_at(a, step):
    offset, flip = step
    return jnp.bitwise_xor(lax.rem(a + offset, 8), flip)


def dress(meta, domains, rows, row_energy, column_energy, blocks, steps, total, chunks, last):
    count = len(blocks)
    width = count * BLK
    has_total = total is not None

    def kernel(*refs):
        meta, domains, rows_high, rows_low, row_energy, column_energy = refs[:6]
        columns = refs[6 : 6 + count]
        refs = refs[6 + count :]
        before = None
        if has_total:
            before, refs = refs[0], refs[1:]
        out, wide, turned_high, turned_low = refs[:4]
        a, z, c = meta[0], meta[1], meta[2]
        core = lax.rem(c, 2)
        for q in range(count):
            slot = jnp.int32(0)
            span = slice(q * BLK, (q + 1) * BLK)
            for fit in range(NPB):
                here = present(domains, z, 2 * tile_at(a, steps[q]) + core, fit)
                block = columns[q][block_rows(jnp.minimum(slot, SLOTS - 1)), :]
                block = jnp.where(here == 1, block, 0.0)
                one, two = split(block)
                own = slice(fit * BLK, (fit + 1) * BLK)
                wide[own, q * BLK : (q + 1) * BLK] = one
                wide[own, width + q * BLK : width + (q + 1) * BLK] = one
                wide[own, 2 * width + q * BLK : 2 * width + (q + 1) * BLK] = two
                one, two = split(block.T)
                turned_high[span, own] = one
                turned_low[span, own] = two
                slot = slot + here
        for n, r in enumerate(chunks):
            span = slice(r * TILE, (r + 1) * TILE)
            direct = dot3(
                (turned_high[...], turned_low[...]), (rows_high[:, span], rows_low[:, span]), ((1,), (0,))
            )
            amps = -direct / (column_energy[...] + row_energy[:, span])
            high, low = split(amps)
            found = lax.dot_general(
                wide[...],
                jnp.concatenate([high, low, high], axis=0),
                (((1,), (0,)), ((), ())),
                preferred_element_type=f32,
            )
            if has_total:
                found = found + before[:, span]
            if not last:
                out[:, span] = found
                continue
            dense = refs[4].at[n]
            dense[...] = found
            orbital = 2 * c + r if r < 2 else 2 * (c + 1 - 2 * core) + r - 2
            for half in range(2):
                lanes = slice(half * BLK, (half + 1) * BLK)
                fits = [jnp.int32(0)] * SLOTS
                slot = jnp.int32(0)
                for fit in range(NPB):
                    here = present(domains, orbital, 2 * a + half, fit)
                    for s in range(SLOTS):
                        fits[s] = jnp.where((here == 1) & (slot == s), fit, fits[s])
                    slot = slot + here
                for k in range(24):
                    o = lax.rem(k // 3 + 8 - z, 8)
                    source = pl.ds(pl.multiple_of(fits[k // 4] * BLK + (k % 4) * 32, 32), 32)
                    out[o, n, (k % 3) * 32 : (k % 3 + 1) * 32, lanes] = dense[source, lanes]

    scratch = [
        pltpu.VMEM((NAUX, 3 * width), bf16),
        pltpu.VMEM((width, NAUX), bf16),
        pltpu.VMEM((width, NAUX), bf16),
    ]
    if last:
        out_shape = jax.ShapeDtypeStruct((8, len(chunks), PIECE, TILE), f32)
        scratch.append(pltpu.VMEM((len(chunks), NAUX, TILE), f32))
    else:
        out_shape = jax.ShapeDtypeStruct((NAUX, 4 * TILE), f32)
    operands = [meta, domains, *rows, row_energy, column_energy, *blocks]
    in_specs = [SMEM] * 2 + [VMEM] * (4 + count)
    if has_total:
        operands.append(total)
        in_specs.append(VMEM)
    return pl.pallas_call(
        kernel,
        out_shape=out_shape,
        in_specs=in_specs,
        out_specs=VMEM,
        scratch_shapes=scratch,
        compiler_params=params(20),
        cost_estimate=cost(12 * NAUX * width * len(chunks) * TILE, 14),
        name="dress",
    )(*operands)


def blocks_of(store, domains, orbital, first_block, put):
    for half in range(2):
        slot = jnp.int32(0)
        lanes = slice(half * BLK, (half + 1) * BLK)
        for fit in range(NPB):
            here = present(domains, orbital, first_block + half, fit)
            block = store[block_rows(jnp.minimum(slot, SLOTS - 1)), lanes]
            put(half, fit, jnp.where(here == 1, block, 0.0))
            slot = slot + here


def pass_on(value, *after):
    def kernel(*refs):
        refs[-1][...] = refs[0][...]

    return pl.pallas_call(
        kernel,
        out_shape=jax.ShapeDtypeStruct(value.shape, value.dtype),
        in_specs=[VMEM] + [pl.BlockSpec(memory_space=pl.ANY)] * len(after),
        out_specs=VMEM,
        compiler_params=params(4),
        cost_estimate=cost(0, 1),
        name="pass_on",
    )(value, *after)


def spread_far(meta, domains, arrays, parts):
    def kernel(meta, domains, *refs):
        arrays, (far_high, far_low, packed) = refs[:4], refs[4:]
        a, z, c = meta[0], meta[1], meta[2]
        for f in range(2):
            for where, which, part in parts:
                place = pl.ds(pl.multiple_of(tile_at(a, where) * PIECE, 8), PIECE)
                packed.at[f][place, :] = arrays[which][part, f]

            def put(half, fit, block, f=f):
                own = slice(fit * BLK, (fit + 1) * BLK)
                lanes = slice(f * TILE + half * BLK, f * TILE + (half + 1) * BLK)
                far_high[own, lanes], far_low[own, lanes] = split(block)

            blocks_of(packed.at[f], domains, 2 * c + f, 2 * z, put)

    shape = jax.ShapeDtypeStruct((NAUX, 2 * TILE), bf16)
    return pl.pallas_call(
        kernel,
        out_shape=(shape, shape),
        in_specs=[SMEM, SMEM] + [VMEM] * 4,
        out_specs=(VMEM, VMEM),
        scratch_shapes=[pltpu.VMEM((2, PRES, TILE), f32)],
        compiler_params=params(56),
        cost_estimate=cost(0, 4),
        name="spread_far",
    )(meta, domains, *arrays)


def finish(meta, domains, occ_energy, vir_near, col_energy, far, near, groups, filled):
    near_parts, near_arrays = near
    n_near = len(near_arrays)
    has_filled = filled is not None

    def kernel(*refs):
        meta, domains, occ, vir_near, col_energy, far_high, far_low = refs[:7]
        near_refs = refs[7 : 7 + n_near]
        out, packed, high, low = refs[7 + n_near + (1 if has_filled else 0) :]
        a, z, c = meta[0], meta[1], meta[2]
        step = pl.program_id(0)
        upper, e = step // 2, lax.rem(step, 2)

        def rows_of(place):
            return pl.ds(pl.multiple_of(place * PIECE, 8), PIECE)

        orbital = 2 * jnp.bitwise_xor(c, groups[0] + upper * (groups[1] - groups[0])) + e
        for offset, which, part in near_parts:
            place = rows_of(lax.rem(z + offset, 8))
            if part is not None:
                packed[place, :] = near_refs[which][part + (upper, e)]
                continue
            for n, (w, p) in enumerate(which):

                @pl.when(upper == n)
                def _(w=w, p=p, place=place):
                    packed[place, :] = near_refs[w][p + (e,)]

        def put(half, fit, block):
            own = slice(fit * BLK, (fit + 1) * BLK)
            span = slice(half * BLK, (half + 1) * BLK)
            high[span, own], low[span, own] = split(block.T)

        blocks_of(packed, domains, orbital, 2 * a, put)
        residual = dot3((high[...], low[...]), (far_high[...], far_low[...]), ((1,), (0,)))
        energy = (vir_near[...] - occ[orbital]) + col_energy[...]
        result = (residual * (-SCALE)) / energy
        for j in range(2):
            for b in range(2):
                lanes = slice(j * TILE + b * BLK, j * TILE + (b + 1) * BLK)
                out[pl.ds(2 * b + j, TILE, stride=4), :] = result[:, lanes]

    def place(n, meta, domains, occ):
        pair = jnp.bitwise_xor(meta[2], groups[0] + (n // 2) * (groups[1] - groups[0]))
        return 2 * pair + lax.rem(n, 2), 0

    operands = [meta, domains, occ_energy, vir_near, col_energy, *far, *near_arrays]
    in_specs = [VMEM] * (4 + n_near)
    aliases = {}
    if has_filled:
        aliases = {len(operands): 0}
        operands.append(filled)
        in_specs.append(pl.BlockSpec(memory_space=pl.ANY))
    return pl.pallas_call(
        kernel,
        out_shape=jax.ShapeDtypeStruct((O * TILE * 4, BLK), f32),
        grid_spec=pltpu.PrefetchScalarGridSpec(
            num_scalar_prefetch=3,
            grid=(4,),
            in_specs=in_specs,
            out_specs=pl.BlockSpec((TILE * 4, BLK), place),
            scratch_shapes=[
                pltpu.VMEM((PRES, TILE), f32),
                pltpu.VMEM((TILE, NAUX), bf16),
                pltpu.VMEM((TILE, NAUX), bf16),
            ],
        ),
        input_output_aliases=aliases,
        compiler_params=params(56, 1),
        cost_estimate=cost(6 * NAUX * 1024 * 512, 8),
        name="finish",
    )(*operands)


def body(factors, domains, occ_energy, vir_energy):
    a = lax.axis_index("va")
    z = lax.axis_index("vb")
    c = lax.axis_index("aux")
    core = c % 2
    meta = jnp.stack([a, z, c]).astype(jnp.int32)
    flags = domains.reshape(-1)
    flat = factors.reshape(NAUX * O, TILE)

    column = pick_column(meta, flags, flat)
    right, left, y_own = send(column, "x+"), send(column, "x-"), send(column, "y")
    rows_high, rows_low, piece = prepare(meta, flags, flat)
    rows = (rows_high, rows_low)
    piece, near_right, near_left = lax.optimization_barrier((piece, right, left))
    beyond = send(jnp.where(core == 0, near_right, near_left), "x_by_core")
    y_right, y_left, y_beyond = (send(block, "y") for block in (near_right, near_left, beyond))
    vir_near = lax.dynamic_slice_in_dim(vir_energy, a * TILE, TILE)
    occ_pairs = occ_energy.reshape(4, 2)
    occ_rows = jnp.concatenate([occ_pairs[c], occ_pairs[c ^ 1]])
    row_energy = (vir_near[None, :] - occ_rows[:, None]).reshape(1, 4 * TILE)
    tiles = jnp.stack([(a + d) % 8 ^ f for d, f in ((0, 0), (0, 1), (6, 0), (2, 0), (6, 1), (2, 1), (4, 0), (4, 1))])
    energies = (vir_energy.reshape(8, 2, BLK)[:, core][tiles] - occ_energy[z]).reshape(8 * BLK, 1)

    def add(n, blocks, steps, total, chunks=(0, 1, 2, 3), last=False):
        part = energies[2 * n * BLK : 2 * (n + 1) * BLK]
        return dress(meta, flags, rows, row_energy, part, blocks, steps, total, chunks, last)

    total = add(0, [column, y_own], [(0, 0), (0, 1)], None)
    total = add(1, [right, left], [(6, 0), (2, 0)], total)
    total = add(2, [y_right, y_left], [(6, 1), (2, 1)], total)
    final = ([beyond, y_beyond], [(4, 0), (4, 1)], total)
    give = add(3, *final, chunks=(2, 3), last=True)

    first = send(give[3:5], "core")
    rest = send(jnp.concatenate([give[:3], give[5:]]), "core")
    keep = add(3, *final, chunks=(0, 1), last=True)
    got = [rest[0], rest[1], rest[2], first[0], first[1], rest[3], rest[4], rest[5]]
    plus = send(keep[3] + got[3], "z+")
    minus = send(keep[4] + got[4], "z-")
    minus = send(keep[5] + got[5] + minus, "z-")
    plus = send(keep[2] + got[2] + plus, "z+")
    minus = send(keep[6] + got[6] + minus, "z-")
    plus = send(keep[1] + got[1] + plus, "z+")
    minus = send(keep[7] + got[7] + minus, "z-")
    summed = (keep[0] + got[0]) + (plus + minus)
    combined = piece + 2.0 * summed

    turned, across = send(combined, "turn"), send(combined, "y_hi")
    combined, turned, across = lax.optimization_barrier((combined, turned, across))

    both = jnp.stack([combined, across])
    plus1, minus1 = send(both, "z+"), send(both, "z-")
    far_pair = jnp.stack([turned, send(turned, "y_lo")])
    plus2, minus2 = send(plus1, "z+"), send(minus1, "z-")
    moved = pass_on(far_pair, plus1, minus1)
    far_right, far_left = send(moved, "x+"), send(moved, "x-")
    plus2, minus2, far_right, far_left = lax.optimization_barrier((plus2, minus2, far_right, far_left))
    plus3, minus3 = send(plus2, "z+"), send(minus2, "z-")
    moved = pass_on(jnp.where(core == 0, far_right, far_left), plus2, minus2)
    far_beyond = send(moved, "x_by_core")
    plus3, minus3, far_beyond = lax.optimization_barrier((plus3, minus3, far_beyond))
    far_parts = []
    for which, offset in enumerate([0, 6, 2, 4]):
        far_parts += [((offset, 0), which, 0), ((offset, 1), which, 1)]
    far = spread_far(meta, flags, [far_pair, far_right, far_left, far_beyond], far_parts)
    early = send(jnp.stack([both, plus1, minus1, plus2, minus2]), "core")
    plus4, minus4 = send(plus3[0], "z+"), send(minus3[1], "z-")
    late = send(jnp.stack([plus3, minus3, jnp.stack([plus4, minus4])]), "core")
    ring = [both, plus1, minus1, plus2, minus2, plus3, minus3, plus4, minus4]
    offsets = [0, 7, 1, 6, 2, 5, 3]
    ring_parts = [(o, n, ()) for n, o in enumerate(offsets)] + [(4, ((7, ()), (8, ())), None)]
    swap_parts = [(o, 0, (n,)) if n < 5 else (o, 1, (n - 5,)) for n, o in enumerate(offsets)] + [(4, 1, (2,))]
    pair_energy = lax.dynamic_slice_in_dim(vir_energy, z * TILE, TILE)[None, :] - occ_pairs[c][:, None]

    def rows_for(near, groups, filled):
        return finish(
            meta,
            flags,
            occ_energy,
            vir_near.reshape(TILE, 1),
            pair_energy.reshape(1, 2 * TILE),
            far,
            near,
            groups,
            filled,
        )

    filled = rows_for((ring_parts, ring), (0, 2), None)
    filled = rows_for((swap_parts, [early, late]), (1, 3), filled)
    return filled.reshape(O, TILE, 2, 2, BLK).transpose(0, 1, 3, 2, 4).reshape(O, TILE, 2, TILE)


def solution(mesh):
    placed = (P(None, None, "va"), P(), P(), P())
    return jax.shard_map(
        body, mesh=mesh, in_specs=placed, out_specs=P(None, "va", "aux", "vb"), check_vma=False
    )
```

```python
import math

import jax
import jax.numpy as jnp
from jax import lax
from jax.experimental import pallas as pl
from jax.experimental.pallas import tpu as pltpu
from jax.sharding import PartitionSpec as P

O = 8
V = 2048
NAUX = 1024
BLK = 128
NPB = 8
NVB = 16
SLOTS = 6
PRES = SLOTS * BLK
PIECE = PRES // 8
TILE = 256
SCALE = 8.0 * O * V / math.sqrt(NAUX)
AXES = ("va", "vb", "aux")
f32 = jnp.float32
bf16 = jnp.bfloat16


def route(move):
    pairs = []
    for a in range(8):
        for b in range(8):
            for c in range(4):
                A, B, C = move(a, b, c)
                pairs.append(((a * 8 + b) * 4 + c, (A * 8 + B) * 4 + C))
    return pairs


def shift_x(a, d):
    return ((a // 2 + d) % 4) * 2 + a % 2


def y_by_core(a, b, c):
    y = (c // 2) * 2 + a % 2
    y = (y + (1 if c % 2 == 0 else -1)) % 4
    return (a // 2) * 2 + y % 2, b, (y // 2) * 2 + c % 2


ROUTES = {
    "x+": route(lambda a, b, c: (shift_x(a, 1), b, c)),
    "x-": route(lambda a, b, c: (shift_x(a, -1), b, c)),
    "x2": route(lambda a, b, c: (shift_x(a, 2), b, c)),
    "y": route(y_by_core),
    "y_lo": route(lambda a, b, c: (a ^ 1, b, c)),
    "y_hi": route(lambda a, b, c: (a, b, c ^ 2)),
    "z+": route(lambda a, b, c: (a, (b + 1) % 8, c)),
    "z-": route(lambda a, b, c: (a, (b - 1) % 8, c)),
    "x_by_core": route(lambda a, b, c: (shift_x(a, 1 - 2 * (c % 2)), b, c)),
    "core": route(lambda a, b, c: (a, b, c ^ 1)),
    "turn": route(lambda a, b, c: (b, a, c)),
}


def send(value, way):
    return lax.ppermute(value, AXES, ROUTES[way])


def split(value):
    high = value.astype(bf16)
    low = (value - high.astype(f32)).astype(bf16)
    return high, low


def dot3(left, right, dims):
    def one(l, r):
        return lax.dot_general(l, r, (dims, ((), ())), preferred_element_type=f32)

    return one(left[0], right[0]) + (one(left[0], right[1]) + one(left[1], right[0]))


def present(domains, orbital, block, fit):
    return domains[(orbital * NVB + block) * NPB + fit]


SMEM = pl.BlockSpec(memory_space=pltpu.SMEM)
VMEM = pl.BlockSpec(memory_space=pltpu.VMEM)


def params(mib, grid=0):
    order = {"dimension_semantics": ("arbitrary",) * grid} if grid else {}
    return pltpu.CompilerParams(vmem_limit_bytes=mib * 1024 * 1024, **order)


def cost(flops, mib):
    return pl.CostEstimate(flops=flops, bytes_accessed=mib * 1024 * 1024, transcendentals=0)


def block_rows(slot):
    return pl.ds(pl.multiple_of(slot * BLK, BLK), BLK)


def load(x, fit, orbital):
    return x[pl.ds(fit * BLK * O + orbital, BLK, stride=O), :]


def pack(target, x, domains, orbital, block):
    slot = jnp.int32(0)
    for fit in range(NPB):
        here = present(domains, orbital, block, fit)

        @pl.when(here == 1)
        def _(slot=slot, fit=fit):
            target[block_rows(slot), :] = load(x, fit, orbital)

        slot = slot + here


def pick_column(meta, domains, factors):
    def kernel(meta, domains, x, column):
        pack(column, x, domains, meta[1], 2 * meta[0] + lax.rem(meta[2], 2))

    return pl.pallas_call(
        kernel,
        out_shape=jax.ShapeDtypeStruct((PRES, BLK), f32),
        grid_spec=pltpu.PrefetchScalarGridSpec(
            num_scalar_prefetch=2,
            grid=(1,),
            in_specs=[pl.BlockSpec((NAUX * O, BLK), lambda n, meta, domains: (0, lax.rem(meta[2], 2)))],
            out_specs=pl.BlockSpec((PRES, BLK), lambda n, meta, domains: (0, 0)),
        ),
        compiler_params=params(56, 1),
        cost_estimate=cost(0, 5),
        name="pick_column",
    )(meta, domains, factors)


def prepare(meta, domains, factors):
    def kernel(meta, domains, x, rows_high, rows_low, piece, packed):
        a, z, c = meta[0], meta[1], meta[2]
        core = lax.rem(c, 2)
        for h in range(2):

            @pl.when(pl.program_id(0) == h)
            def _(h=h):
                lanes = slice(h * BLK, (h + 1) * BLK)
                for e in range(2):
                    store = packed.at[2 * e + h]
                    pack(store, x, domains, 2 * c + e, 2 * a + h)
                for r in range(4):
                    orbital = 2 * c + r if r < 2 else 2 * (c + 1 - 2 * core) + r - 2
                    for fit in range(NPB):
                        here = present(domains, orbital, 2 * a + h, fit).astype(f32)
                        high, low = split(load(x, fit, orbital) * here)
                        place = (slice(fit * BLK, (fit + 1) * BLK), slice(r * TILE + h * BLK, r * TILE + (h + 1) * BLK))
                        rows_high[place] = high
                        rows_low[place] = low
                window = pl.ds(pl.multiple_of(z * PIECE, 8), PIECE)
                for e in range(2):
                    piece[e, :, lanes] = packed[2 * e + h, window, :]

    return pl.pallas_call(
        kernel,
        out_shape=(
            jax.ShapeDtypeStruct((NAUX, 4 * TILE), bf16),
            jax.ShapeDtypeStruct((NAUX, 4 * TILE), bf16),
            jax.ShapeDtypeStruct((2, PIECE, TILE), f32),
        ),
        grid_spec=pltpu.PrefetchScalarGridSpec(
            num_scalar_prefetch=2,
            grid=(2,),
            in_specs=[pl.BlockSpec((NAUX * O, BLK), lambda n, meta, domains: (0, n))],
            out_specs=(
                pl.BlockSpec((NAUX, 4 * TILE), lambda n, meta, domains: (0, 0)),
                pl.BlockSpec((NAUX, 4 * TILE), lambda n, meta, domains: (0, 0)),
                pl.BlockSpec((2, PIECE, TILE), lambda n, meta, domains: (0, 0, 0)),
            ),
            scratch_shapes=[pltpu.VMEM((4, PRES, BLK), f32)],
        ),
        compiler_params=params(26, 1),
        cost_estimate=cost(0, 14),
        name="prepare",
    )(meta, domains, factors)


def tile_at(a, step):
    offset, flip = step
    return jnp.bitwise_xor(lax.rem(a + offset, 8), flip)


def dress(meta, domains, rows, row_energy, column_energy, blocks, steps, total, chunks, last):
    count = len(blocks)
    width = count * BLK
    has_total = total is not None

    def kernel(*refs):
        meta, domains, rows_high, rows_low, row_energy, column_energy = refs[:6]
        columns = refs[6 : 6 + count]
        refs = refs[6 + count :]
        before = None
        if has_total:
            before, refs = refs[0], refs[1:]
        out, wide, turned_high, turned_low = refs[:4]
        a, z, c = meta[0], meta[1], meta[2]
        core = lax.rem(c, 2)
        for q in range(count):
            slot = jnp.int32(0)
            span = slice(q * BLK, (q + 1) * BLK)
            for fit in range(NPB):
                here = present(domains, z, 2 * tile_at(a, steps[q]) + core, fit)
                block = columns[q][block_rows(jnp.minimum(slot, SLOTS - 1)), :]
                block = jnp.where(here == 1, block, 0.0)
                one, two = split(block)
                own = slice(fit * BLK, (fit + 1) * BLK)
                wide[own, q * BLK : (q + 1) * BLK] = one
                wide[own, width + q * BLK : width + (q + 1) * BLK] = one
                wide[own, 2 * width + q * BLK : 2 * width + (q + 1) * BLK] = two
                one, two = split(block.T)
                turned_high[span, own] = one
                turned_low[span, own] = two
                slot = slot + here
        for n, r in enumerate(chunks):
            span = slice(r * TILE, (r + 1) * TILE)
            direct = dot3(
                (turned_high[...], turned_low[...]), (rows_high[:, span], rows_low[:, span]), ((1,), (0,))
            )
            amps = -direct / (column_energy[...] + row_energy[:, span])
            high, low = split(amps)
            found = lax.dot_general(
                wide[...],
                jnp.concatenate([high, low, high], axis=0),
                (((1,), (0,)), ((), ())),
                preferred_element_type=f32,
            )
            if has_total:
                found = found + before[:, span]
            if not last:
                out[:, span] = found
                continue
            dense = refs[4].at[n]
            dense[...] = found
            orbital = 2 * c + r if r < 2 else 2 * (c + 1 - 2 * core) + r - 2
            for half in range(2):
                lanes = slice(half * BLK, (half + 1) * BLK)
                fits = [jnp.int32(0)] * SLOTS
                slot = jnp.int32(0)
                for fit in range(NPB):
                    here = present(domains, orbital, 2 * a + half, fit)
                    for s in range(SLOTS):
                        fits[s] = jnp.where((here == 1) & (slot == s), fit, fits[s])
                    slot = slot + here
                for k in range(24):
                    o = lax.rem(k // 3 + 8 - z, 8)
                    source = pl.ds(pl.multiple_of(fits[k // 4] * BLK + (k % 4) * 32, 32), 32)
                    out[o, n, (k % 3) * 32 : (k % 3 + 1) * 32, lanes] = dense[source, lanes]

    scratch = [
        pltpu.VMEM((NAUX, 3 * width), bf16),
        pltpu.VMEM((width, NAUX), bf16),
        pltpu.VMEM((width, NAUX), bf16),
    ]
    if last:
        out_shape = jax.ShapeDtypeStruct((8, len(chunks), PIECE, TILE), f32)
        scratch.append(pltpu.VMEM((len(chunks), NAUX, TILE), f32))
    else:
        out_shape = jax.ShapeDtypeStruct((NAUX, 4 * TILE), f32)
    operands = [meta, domains, *rows, row_energy, column_energy, *blocks]
    in_specs = [SMEM] * 2 + [VMEM] * (4 + count)
    if has_total:
        operands.append(total)
        in_specs.append(VMEM)
    return pl.pallas_call(
        kernel,
        out_shape=out_shape,
        in_specs=in_specs,
        out_specs=VMEM,
        scratch_shapes=scratch,
        compiler_params=params(20),
        cost_estimate=cost(12 * NAUX * width * len(chunks) * TILE, 14),
        name="dress",
    )(*operands)


def blocks_of(store, domains, orbital, first_block, put):
    for half in range(2):
        slot = jnp.int32(0)
        lanes = slice(half * BLK, (half + 1) * BLK)
        for fit in range(NPB):
            here = present(domains, orbital, first_block + half, fit)
            block = store[block_rows(jnp.minimum(slot, SLOTS - 1)), lanes]
            put(half, fit, jnp.where(here == 1, block, 0.0))
            slot = slot + here


def pass_on(value, *after):
    def kernel(*refs):
        refs[-1][...] = refs[0][...]

    return pl.pallas_call(
        kernel,
        out_shape=jax.ShapeDtypeStruct(value.shape, value.dtype),
        in_specs=[VMEM] + [pl.BlockSpec(memory_space=pl.ANY)] * len(after),
        out_specs=VMEM,
        compiler_params=params(4),
        cost_estimate=cost(0, 1),
        name="pass_on",
    )(value, *after)


def spread_far(meta, domains, arrays, parts):
    def kernel(meta, domains, *refs):
        arrays, (far_high, far_low, packed) = refs[:4], refs[4:]
        a, z, c = meta[0], meta[1], meta[2]
        for f in range(2):
            for where, which, part in parts:
                place = pl.ds(pl.multiple_of(tile_at(a, where) * PIECE, 8), PIECE)
                packed.at[f][place, :] = arrays[which][part, f]

            def put(half, fit, block, f=f):
                own = slice(fit * BLK, (fit + 1) * BLK)
                lanes = slice(f * TILE + half * BLK, f * TILE + (half + 1) * BLK)
                far_high[own, lanes], far_low[own, lanes] = split(block)

            blocks_of(packed.at[f], domains, 2 * c + f, 2 * z, put)

    shape = jax.ShapeDtypeStruct((NAUX, 2 * TILE), bf16)
    return pl.pallas_call(
        kernel,
        out_shape=(shape, shape),
        in_specs=[SMEM, SMEM] + [VMEM] * 4,
        out_specs=(VMEM, VMEM),
        scratch_shapes=[pltpu.VMEM((2, PRES, TILE), f32)],
        compiler_params=params(56),
        cost_estimate=cost(0, 4),
        name="spread_far",
    )(meta, domains, *arrays)


def finish(meta, domains, occ_energy, vir_near, col_energy, far, near):
    near_parts, near_arrays = near
    n_near = len(near_arrays)

    def kernel(*refs):
        meta, domains, occ, vir_near, col_energy, far_high, far_low = refs[:7]
        near_refs = refs[7 : 7 + n_near]
        out, packed, high, low = refs[7 + n_near :]
        a, z, c = meta[0], meta[1], meta[2]
        step = pl.program_id(0)
        swapped, upper, e = step // 4, lax.rem(step // 2, 2), lax.rem(step, 2)

        def rows_of(place):
            return pl.ds(pl.multiple_of(place * PIECE, 8), PIECE)

        orbital = 2 * jnp.bitwise_xor(c, 2 * upper + swapped) + e
        for case, parts in enumerate(near_parts):

            @pl.when(swapped == case)
            def _(parts=parts):
                for offset, which, part in parts:
                    place = rows_of(lax.rem(z + offset, 8))
                    if part is not None:
                        packed[place, :] = near_refs[which][part + (upper, e)]
                        continue
                    for n, (w, p) in enumerate(which):

                        @pl.when(upper == n)
                        def _(w=w, p=p, place=place):
                            packed[place, :] = near_refs[w][p + (e,)]

        def put(half, fit, block):
            own = slice(fit * BLK, (fit + 1) * BLK)
            span = slice(half * BLK, (half + 1) * BLK)
            high[span, own], low[span, own] = split(block.T)

        blocks_of(packed, domains, orbital, 2 * a, put)
        residual = dot3((high[...], low[...]), (far_high[...], far_low[...]), ((1,), (0,)))
        energy = (vir_near[...] - occ[orbital]) + col_energy[...]
        result = (residual * (-SCALE)) / energy
        for j in range(2):
            for b in range(2):
                lanes = slice(j * TILE + b * BLK, j * TILE + (b + 1) * BLK)
                out[pl.ds(2 * b + j, TILE, stride=4), :] = result[:, lanes]

    def place(n, meta, domains, occ):
        pair = jnp.bitwise_xor(meta[2], 2 * lax.rem(n // 2, 2) + n // 4)
        return 2 * pair + lax.rem(n, 2), 0

    operands = [meta, domains, occ_energy, vir_near, col_energy, *far, *near_arrays]
    in_specs = [VMEM] * (4 + n_near)
    return pl.pallas_call(
        kernel,
        out_shape=jax.ShapeDtypeStruct((O * TILE * 4, BLK), f32),
        grid_spec=pltpu.PrefetchScalarGridSpec(
            num_scalar_prefetch=3,
            grid=(8,),
            in_specs=in_specs,
            out_specs=pl.BlockSpec((TILE * 4, BLK), place),
            scratch_shapes=[
                pltpu.VMEM((PRES, TILE), f32),
                pltpu.VMEM((TILE, NAUX), bf16),
                pltpu.VMEM((TILE, NAUX), bf16),
            ],
        ),
        compiler_params=params(56, 1),
        cost_estimate=cost(6 * NAUX * 2048 * 512, 12),
        name="finish",
    )(*operands)


def body(factors, domains, occ_energy, vir_energy):
    a = lax.axis_index("va")
    z = lax.axis_index("vb")
    c = lax.axis_index("aux")
    core = c % 2
    meta = jnp.stack([a, z, c]).astype(jnp.int32)
    flags = domains.reshape(-1)
    flat = factors.reshape(NAUX * O, TILE)

    column = pick_column(meta, flags, flat)
    right, left, y_own = send(column, "x+"), send(column, "x-"), send(column, "y")
    rows_high, rows_low, piece = prepare(meta, flags, flat)
    rows = (rows_high, rows_low)
    piece, near_right, near_left = lax.optimization_barrier((piece, right, left))
    beyond = send(jnp.where(core == 0, near_right, near_left), "x_by_core")
    y_right, y_left, y_beyond = (send(block, "y") for block in (near_right, near_left, beyond))
    vir_near = lax.dynamic_slice_in_dim(vir_energy, a * TILE, TILE)
    occ_pairs = occ_energy.reshape(4, 2)
    occ_rows = jnp.concatenate([occ_pairs[c], occ_pairs[c ^ 1]])
    row_energy = (vir_near[None, :] - occ_rows[:, None]).reshape(1, 4 * TILE)
    tiles = jnp.stack([(a + d) % 8 ^ f for d, f in ((0, 0), (0, 1), (6, 0), (2, 0), (6, 1), (2, 1), (4, 0), (4, 1))])
    energies = (vir_energy.reshape(8, 2, BLK)[:, core][tiles] - occ_energy[z]).reshape(8 * BLK, 1)

    def add(n, blocks, steps, total, chunks=(0, 1, 2, 3), last=False):
        part = energies[2 * n * BLK : 2 * (n + 1) * BLK]
        return dress(meta, flags, rows, row_energy, part, blocks, steps, total, chunks, last)

    total = add(0, [column, y_own], [(0, 0), (0, 1)], None)
    total = add(1, [right, left], [(6, 0), (2, 0)], total)
    total = add(2, [y_right, y_left], [(6, 1), (2, 1)], total)
    final = ([beyond, y_beyond], [(4, 0), (4, 1)], total)
    give = add(3, *final, chunks=(2, 3), last=True)

    first = send(give[3:5], "core")
    rest = send(jnp.concatenate([give[:3], give[5:]]), "core")
    keep = add(3, *final, chunks=(0, 1), last=True)
    got = [rest[0], rest[1], rest[2], first[0], first[1], rest[3], rest[4], rest[5]]
    plus = send(keep[3] + got[3], "z+")
    minus = send(keep[4] + got[4], "z-")
    plus, minus = lax.optimization_barrier((plus, minus))
    minus = send(keep[5] + got[5] + minus, "z-")
    plus = send(keep[2] + got[2] + plus, "z+")
    minus = send(keep[6] + got[6] + minus, "z-")
    plus = send(keep[1] + got[1] + plus, "z+")
    minus = send(keep[7] + got[7] + minus, "z-")
    summed = (keep[0] + got[0]) + (plus + minus)
    combined = piece + 2.0 * summed

    turned, across = send(combined, "turn"), send(combined, "y_hi")
    combined, turned, across = lax.optimization_barrier((combined, turned, across))

    both = jnp.stack([combined, across])
    plus1, minus1 = send(both, "z+"), send(both, "z-")
    far_pair = jnp.stack([turned, send(turned, "y_lo")])
    plus2, minus2 = send(plus1, "z+"), send(minus1, "z-")
    moved = pass_on(far_pair, plus1, minus1)
    far_right, far_left = send(moved, "x+"), send(moved, "x-")
    plus2, minus2, far_right, far_left = lax.optimization_barrier((plus2, minus2, far_right, far_left))
    plus3, minus3 = send(plus2, "z+"), send(minus2, "z-")
    moved = pass_on(jnp.where(core == 0, far_right, far_left), plus2, minus2)
    far_beyond = send(moved, "x_by_core")
    plus3, minus3, far_beyond = lax.optimization_barrier((plus3, minus3, far_beyond))
    far_parts = []
    for which, offset in enumerate([0, 6, 2, 4]):
        far_parts += [((offset, 0), which, 0), ((offset, 1), which, 1)]
    far = spread_far(meta, flags, [far_pair, far_right, far_left, far_beyond], far_parts)
    early = send(jnp.stack([both, plus1, minus1, plus2, minus2]), "core")
    plus4, minus4 = send(plus3[0], "z+"), send(minus3[1], "z-")
    late = send(jnp.stack([plus3, minus3, jnp.stack([plus4, minus4])]), "core")
    ring = [both, plus1, minus1, plus2, minus2, plus3, minus3, plus4, minus4]
    offsets = [0, 7, 1, 6, 2, 5, 3]
    ring_parts = [(o, n, ()) for n, o in enumerate(offsets)] + [(4, ((7, ()), (8, ())), None)]
    swap_parts = [(o, 0, (n,)) if n < 5 else (o, 1, (n - 5,)) for n, o in enumerate(offsets)] + [(4, 1, (2,))]
    pair_energy = lax.dynamic_slice_in_dim(vir_energy, z * TILE, TILE)[None, :] - occ_pairs[c][:, None]

    base = len(ring)
    swap_parts = [(o, base + which, part) for o, which, part in swap_parts]
    filled = finish(
        meta,
        flags,
        occ_energy,
        vir_near.reshape(TILE, 1),
        pair_energy.reshape(1, 2 * TILE),
        far,
        ((ring_parts, swap_parts), ring + [early, late]),
    )
    return filled.reshape(O, TILE, 2, 2, BLK).transpose(0, 1, 3, 2, 4).reshape(O, TILE, 2, TILE)


def solution(mesh):
    placed = (P(None, None, "va"), P(), P(), P())
    return jax.shard_map(
        body, mesh=mesh, in_specs=placed, out_specs=P(None, "va", "aux", "vb"), check_vma=False
    )
```
